32 devices in a mesh: row: 4 (over x, core), col: 4 (over z), layer: 2 (over y).
Axes of the slice: x: 2, y: 2, z: 4, core: 2. Of those that a mesh axis runs over, the one named last changes fastest.
Arguments:
- a_tiles: bfloat16 [4096, 16384], P('row', ('layer', 'col')), may hold values from -6 to 6
- a_occupancy: int32 [32, 128], P('row', ('layer', 'col')), may hold values 0 or 1
- b_tiles: bfloat16 [16384, 8192], P(('layer', 'row'), 'col'), may hold values from -0.046875 to 0.046875
- b_occupancy: int32 [128, 64], P(('layer', 'row'), 'col'), may hold values 0 or 1
Outputs:
- product: float32 [4096, 8192], P(('row', 'layer'), 'col')
The draws below stay inside these ranges and needn't reach their ends.
Inputs may be any that keep to these rules, and one draw needn't show every extreme that they name: `a_occupancy`: each entry is 0 (block absent) or 1 (block present). `b_occupancy`: each entry is 0 (block absent) or 1 (block present).
All inputs are finite; a program needn't handle non-finite values.
Results may differ from the reference program's by a relative error of at most 0.0003.
Values may be sent and summed in bfloat16 or wider, within the bound.
No kernel may reach another device: no remote copies, remote signals or barrier semaphores. Data moves between devices by JAX's collectives and lax.ppermute only.
A program may use at most 128 MiB of HBM per device.

```python
import jax
import jax.numpy as jnp

BLOCK = 128
INNER = 16384
M_ROWS = 4096
N_COLS = 8192


def place_ends(entries, own_key, low, high):
    longest = entries.shape.index(max(entries.shape))
    spots = []
    for shift in (0, 1):
        where = [jax.random.randint(jax.random.fold_in(own_key, axis), (), 0, length) for axis, length in enumerate(entries.shape)]
        where[longest] = (where[longest] + shift) % entries.shape[longest]
        spots.append(tuple(where))
    return entries.at[spots[0]].set(low).at[spots[1]].set(high)


def level_of(key, dims, split, least, top_value):
    factor_of = 1.0
    for dim, parts in split:
        heights = jax.random.uniform(jax.random.fold_in(jax.random.fold_in(key, 6), dim), (parts,), jnp.float32, least / len(split), top_value / len(split))
        factor_of = factor_of * jnp.repeat(jnp.exp(heights), dims[dim] // parts).reshape((-1,) + (1,) * (len(dims) - 1 - dim))
    return factor_of


def centred(key, extent, spread, most, cuts=(), kind=jnp.bfloat16):
    entries = spread * jax.random.normal(key, extent, jnp.float32)
    if cuts:
        entries = entries * level_of(key, extent, cuts, -0.22, 0.18)
    return jnp.clip(entries, -most, most).astype(kind)


def setup_inputs(seed: int = 0) -> dict:
    arg_keys = jax.random.split(jax.random.key(seed), 5)
    return {
        "a_tiles": centred(arg_keys[0], (M_ROWS, INNER), 1.0, 6.0, ((0, 4), (1, 8))),
        "a_occupancy": place_ends((jax.random.randint(arg_keys[1], (M_ROWS // BLOCK, INNER // BLOCK), 0, 25) < 11).astype(jnp.int32), jax.random.fold_in(arg_keys[1], 1), 0, 1),
        "b_tiles": centred(arg_keys[2], (INNER, N_COLS), INNER ** -0.5, 0.046875, ((0, 8), (1, 4))),
        "b_occupancy": place_ends((jax.random.randint(arg_keys[3], (INNER // BLOCK, N_COLS // BLOCK), 0, 25) < 11).astype(jnp.int32), jax.random.fold_in(arg_keys[3], 1), 0, 1),
    }


def keep_blocks(values, occupancy):
    height, breadth = values.shape
    tiled = values.reshape(height // BLOCK, BLOCK, breadth // BLOCK, BLOCK)
    flags = occupancy.astype(values.dtype)
    return (tiled * flags[:, None, :, None]).reshape(height, breadth)


def reference(a_tiles, a_occupancy, b_tiles, b_occupancy):
    a_kept = keep_blocks(a_tiles, a_occupancy)
    b_kept = keep_blocks(b_tiles, b_occupancy)
    return jnp.dot(a_kept, b_kept, preferred_element_type=jnp.float32)
```

```python
import functools

import jax
import jax.numpy as jnp
from jax import lax
from jax.experimental import pallas as pl
from jax.experimental.pallas import tpu as pltpu
from jax.sharding import PartitionSpec as P

BLOCK = 128
VMEM_LIMIT = 56 * 1024 * 1024


def keep_blocks(values, occupancy):
    height, breadth = values.shape
    tiled = values.reshape(height // BLOCK, BLOCK, breadth // BLOCK, BLOCK)
    flags = occupancy.astype(values.dtype)
    return (tiled * flags[:, None, :, None]).reshape(height, breadth)


def whole_slab(a_tiles, a_occupancy, b_tiles, b_occupancy):
    a_kept = keep_blocks(a_tiles, a_occupancy)
    b_kept = keep_blocks(b_tiles, b_occupancy)
    partial_value = jnp.dot(
        lax.all_gather(a_kept, "col", axis=1, tiled=True),
        lax.all_gather(b_kept, "row", axis=0, tiled=True),
        preferred_element_type=jnp.float32,
    )
    return lax.psum_scatter(partial_value, "layer", scatter_dimension=0, tiled=True)


def slots_for(blocks):
    if blocks < 16:
        return blocks + 1
    room = (blocks * 7 + 15) // 16 + int(round(1.56 * blocks**0.5))
    return min(blocks, room) + 1


def cuts_for(stops):
    cuts = [0]
    for blocks in stops:
        cuts.append(max(slots_for(blocks), cuts[-1] + 1))
    return cuts


def header_of(occupancy):
    rows, columns = occupancy.shape
    flags = occupancy.astype(jnp.bfloat16)
    return jnp.pad(flags, ((0, BLOCK - rows), (0, BLOCK - columns)))


def pack_kernel(place, count, cuts, turn_ref, flags_ref, header_ref, values_ref, *refs):
    parts, (held, sems) = refs[: len(cuts) - 1], refs[len(cuts) - 1 :]
    held[0] = header_ref[...]

    def step(t, slot):
        row, column, index = place(t, turn_ref[0])
        at_row = pl.multiple_of(row * BLOCK, BLOCK)
        at_column = pl.multiple_of(column * BLOCK, BLOCK)
        held[jnp.minimum(slot, cuts[-1])] = values_ref[pl.ds(at_row, BLOCK), pl.ds(at_column, BLOCK)]
        return slot + flags_ref[index]

    lax.fori_loop(0, count, step, jnp.int32(1), unroll=8)
    copies = [
        pltpu.make_async_copy(held.at[pl.ds(lo, hi - lo)], part, sems.at[i])
        for i, (part, lo, hi) in enumerate(zip(parts, cuts[:-1], cuts[1:]))
    ]
    for copy in copies:
        copy.start()
    for copy in copies:
        copy.wait()


def pack(values, occupancy, turn, place, cuts):
    count = occupancy.size
    return pl.pallas_call(
        functools.partial(pack_kernel, place, count, cuts),
        grid_spec=pltpu.PrefetchScalarGridSpec(
            num_scalar_prefetch=2,
            grid=(),
            in_specs=[pl.BlockSpec(memory_space=pltpu.VMEM)] * 2,
            out_specs=[pl.BlockSpec(memory_space=pl.ANY)] * (len(cuts) - 1),
            scratch_shapes=[
                pltpu.VMEM((cuts[-1] + 1, BLOCK, BLOCK), values.dtype),
                pltpu.SemaphoreType.DMA((len(cuts) - 1,)),
            ],
        ),
        out_shape=[
            jax.ShapeDtypeStruct((hi - lo, BLOCK, BLOCK), values.dtype) for lo, hi in zip(cuts[:-1], cuts[1:])
        ],
        compiler_params=pltpu.CompilerParams(vmem_limit_bytes=VMEM_LIMIT),
        cost_estimate=pl.CostEstimate(flops=0, bytes_accessed=2 * values.size * 2, transcendentals=0),
        name="pack",
    )(turn, occupancy.reshape(-1), header_of(occupancy), values)


def take(parts, cuts, slot, present):
    block = None
    for part, lo, hi in zip(parts, cuts[:-1], cuts[1:]):
        mine = part[jnp.clip(slot - lo, 0, hi - lo - 1)]
        block = mine if block is None else jnp.where(slot >= lo, mine, block)
    return jnp.where(present, block, jnp.zeros_like(block))


def unpack_a_kernel(place, first, rows, k_blocks, blocks, cuts, turn_ref, flags_ref, *refs):
    parts, out_ref = refs[:-1], refs[-1]
    base = pl.program_id(0) * blocks

    def passed(t, slot):
        return slot + flags_ref[base + place(t, turn_ref[0])[2]]

    def step(t, slot):
        flag = flags_ref[base + place(t + first * k_blocks, turn_ref[0])[2]]
        at_row = pl.multiple_of(t // k_blocks * BLOCK, BLOCK)
        at_column = pl.multiple_of(t % k_blocks * BLOCK, BLOCK)
        out_ref[pl.ds(at_row, BLOCK), pl.ds(at_column, BLOCK)] = take(
            [p.at[0] for p in parts], cuts, slot, flag > 0
        )
        return slot + flag

    slot = lax.fori_loop(0, first * k_blocks, passed, jnp.int32(1))
    lax.fori_loop(0, rows * k_blocks, step, slot, unroll=8)


def unpack_a(parts, flags, turn, place, first, rows, k_blocks, cuts):
    shards = parts[0].shape[0]
    return pl.pallas_call(
        functools.partial(unpack_a_kernel, place, first, rows, k_blocks, flags.size // shards, cuts),
        grid_spec=pltpu.PrefetchScalarGridSpec(
            num_scalar_prefetch=2,
            grid=(shards,),
            in_specs=[pl.BlockSpec((1,) + p.shape[1:], lambda s, *_: (s, 0, 0, 0)) for p in parts],
            out_specs=pl.BlockSpec((rows * BLOCK, k_blocks * BLOCK), lambda s, *_: (0, s)),
        ),
        out_shape=jax.ShapeDtypeStruct((rows * BLOCK, shards * k_blocks * BLOCK), parts[0].dtype),
        compiler_params=pltpu.CompilerParams(vmem_limit_bytes=VMEM_LIMIT),
        cost_estimate=pl.CostEstimate(
            flops=0, bytes_accessed=4 * shards * rows * k_blocks * BLOCK * BLOCK, transcendentals=0
        ),
        name="unpack_a",
    )(turn, flags, *parts)


def unpack_b_kernel(k_blocks, columns, first, wide, cuts, shard_ref, flags_ref, *refs):
    parts, (out_ref, counter) = refs[: len(cuts) - 1], refs[-2:]

    def flag_of(t):
        return flags_ref[t % k_blocks * columns + t // k_blocks]

    @pl.when(pl.program_id(0) == 0)
    def _():
        counter[0] = lax.fori_loop(0, first * k_blocks, lambda t, slot: slot + flag_of(t), jnp.int32(1))

    start = (first + pl.program_id(0) * wide) * k_blocks

    def step(t, slot):
        flag = flag_of(start + t)
        at_row = pl.multiple_of(t % k_blocks * BLOCK, BLOCK)
        at_column = pl.multiple_of(t // k_blocks * BLOCK, BLOCK)
        out_ref[pl.ds(at_row, BLOCK), pl.ds(at_column, BLOCK)] = take(parts, cuts, slot, flag > 0)
        return slot + flag

    counter[0] = lax.fori_loop(0, wide * k_blocks, step, counter[0], unroll=8)


def unpack_b(parts, flags, shard, shards, first, stop, k_blocks, columns, cuts, into):
    wide = 2 if (stop - first) % 2 == 0 else 1
    n = len(parts)
    in_specs = [pl.BlockSpec(p.shape, lambda s, *_: (0, 0, 0)) for p in parts]
    operands = [*parts]
    if into is not None:
        in_specs.append(pl.BlockSpec(memory_space=pl.ANY))
        operands.append(into)
    return pl.pallas_call(
        functools.partial(unpack_b_kernel, k_blocks, columns, first, wide, cuts),
        grid_spec=pltpu.PrefetchScalarGridSpec(
            num_scalar_prefetch=2,
            grid=((stop - first) // wide,),
            in_specs=in_specs,
            out_specs=pl.BlockSpec((k_blocks * BLOCK, wide * BLOCK), lambda s, shard, *_: (shard[0], s)),
            scratch_shapes=[pltpu.SMEM((1,), jnp.int32)],
        ),
        out_shape=jax.ShapeDtypeStruct((shards * k_blocks * BLOCK, (stop - first) * BLOCK), parts[0].dtype),
        input_output_aliases={} if into is None else {2 + n: 0},
        compiler_params=pltpu.CompilerParams(vmem_limit_bytes=VMEM_LIMIT),
        cost_estimate=pl.CostEstimate(
            flops=0, bytes_accessed=4 * (stop - first) * k_blocks * BLOCK * BLOCK, transcendentals=0
        ),
        name="unpack_b",
    )(shard, flags, *operands)


def largest_over(value, axis, size):
    step = 1
    while step < size:
        value = jnp.maximum(value, lax.ppermute(value, axis, [(i, i ^ step) for i in range(size)]))
        step *= 2
    return value


def coded(values):
    height, breadth = values.shape
    tiled = values.reshape(height // BLOCK, BLOCK, breadth)
    top = jnp.max(jnp.abs(tiled), axis=1, keepdims=True)
    factor = jnp.where(top > 0, 32767.0 / top, 0.0)
    return jnp.round(tiled * factor).astype(jnp.int16), top * (1.0 / 32767.0)


def per_device(sizes, a_tiles, a_occupancy, b_tiles, b_occupancy):
    rows, cols, layers = sizes
    me_row, me_layer = lax.axis_index("row"), lax.axis_index("layer")
    a_rows, a_k = a_occupancy.shape
    b_k, b_columns = b_occupancy.shape
    piece = a_rows // layers

    def a_place(t, layer):
        row, k = t // a_k, t % a_k
        at = lax.rem(row + (layer + 1) * piece, a_rows)
        return at, k, at * a_k + k

    def b_place(t, _):
        column, k = t // b_k, t % b_k
        return k, column, k * b_columns + column

    given = a_rows - piece
    row_stops = [given, given + (piece + 1) // 2, a_rows] if piece > 1 else [given, a_rows]
    row_stops = [r for r in row_stops if r > 0]
    column_stops = [b_columns // 2, b_columns] if b_columns % 2 == 0 else [b_columns]
    a_cuts = cuts_for([r * a_k for r in row_stops])
    b_cuts = cuts_for([c * b_k for c in column_stops])

    turn = me_layer.astype(jnp.int32).reshape(1)
    a_parts = pack(a_tiles, a_occupancy, turn, a_place, a_cuts)
    b_parts = pack(b_tiles, b_occupancy, turn, b_place, b_cuts)

    a_turned = jnp.roll(a_occupancy, -(me_layer + 1) * piece, axis=0)
    over = jnp.zeros((), jnp.bool_)
    for stop, cut in zip(row_stops, a_cuts[1:]):
        over |= jnp.sum(a_turned[:stop]) > cut - 1
    for stop, cut in zip(column_stops, b_cuts[1:]):
        over |= jnp.sum(b_occupancy[:, :stop]) > cut - 1
    over = jnp.broadcast_to(over.astype(jnp.float32), (8, BLOCK))
    for axis, size in zip(("row", "layer", "col"), (rows, layers, cols)):
        over = largest_over(over, axis, size)

    a_lists = [lax.all_gather(p, "col", axis=0) for p in a_parts]
    a_flags = a_lists[0][:, 0, :a_rows, :a_k].astype(jnp.int32).reshape(-1)

    pair = 2 if rows % 2 == 0 else 1
    b_lists = []
    for hop in range(rows // pair):
        there = [(r, (r + pair * hop) % rows) for r in range(rows)]
        mine = b_parts if hop == 0 else [lax.ppermute(p, "row", there) for p in b_parts]
        b_lists.append((lax.rem(me_row - pair * hop + rows, rows), mine))
        if pair == 2:
            swap = [(r, r ^ 1) for r in range(rows)]
            b_lists.append((b_lists[-1][0] ^ 1, [lax.ppermute(p, "row", swap) for p in mine]))

    b_halves = []
    for h, stop in enumerate(column_stops):
        first = column_stops[h - 1] if h else 0
        dense = None
        for shard, lists in b_lists:
            flags = lists[0][0, :b_k, :b_columns].astype(jnp.int32).reshape(-1)
            dense = unpack_b(
                lists[: h + 1], flags, shard.astype(jnp.int32).reshape(1), rows, first, stop, b_k, b_columns,
                b_cuts[: h + 2], dense,
            )
        b_halves.append(dense)

    totals = [[None] * len(column_stops) for _ in row_stops]
    for g, stop in enumerate(row_stops):
        first = row_stops[g - 1] if g else 0
        a_dense = unpack_a(a_lists[: g + 1], a_flags, turn, a_place, first, stop - first, a_k, a_cuts[: g + 2])
        for h, b_dense in enumerate(b_halves):
            totals[g][h] = jnp.dot(a_dense, b_dense, preferred_element_type=jnp.float32)

    own = totals
    if given:
        own = totals[1:]
        for h in range(len(column_stops)):
            received = 0.0
            for q in range(layers - 1):
                codes, factors = coded(totals[0][h][q * piece * BLOCK : (q + 1) * piece * BLOCK])
                there = [(i, (i + 1 + q) % layers) for i in range(layers)]
                codes, factors = lax.ppermute(codes, "layer", there), lax.ppermute(factors, "layer", there)
                received += codes.astype(jnp.float32) * factors
            received = received.reshape(piece * BLOCK, -1)
            for g in range(len(own)):
                first, stop = row_stops[g] - given, row_stops[g + 1] - given
                own[g][h] = own[g][h] + received[first * BLOCK : stop * BLOCK]
    product = jnp.concatenate([jnp.concatenate(line, axis=1) for line in own], axis=0)
    return lax.cond(
        over[0, 0] > 0,
        lambda: whole_slab(a_tiles, a_occupancy, b_tiles, b_occupancy),
        lambda: product,
    )


def solution(mesh):
    sizes = tuple(mesh.shape[axis] for axis in ("row", "col", "layer"))
    in_specs = (
        P("row", ("layer", "col")),
        P("row", ("layer", "col")),
        P(("layer", "row"), "col"),
        P(("layer", "row"), "col"),
    )
    out_specs = P(("row", "layer"), "col")
    return jax.shard_map(
        functools.partial(per_device, sizes), mesh=mesh, in_specs=in_specs, out_specs=out_specs, check_vma=False
    )
```

```python
import functools
import math
import typing

import jax
import jax.numpy as jnp
from jax import lax
from jax.experimental import pallas as pl
from jax.experimental.pallas import tpu as pltpu
from jax.sharding import PartitionSpec as P

BLOCK = 128
VMEM_LIMIT = 56 * 1024 * 1024
TILE_ROOM = 256 * 16
SMALL = pl.CostEstimate(flops=1, bytes_accessed=1, transcendentals=0)
LARGE = pl.CostEstimate(flops=10**12, bytes_accessed=1, transcendentals=0)


def keep_blocks(values, occupancy):
    height, breadth = values.shape
    tiled = values.reshape(height // BLOCK, BLOCK, breadth // BLOCK, BLOCK)
    flags = occupancy.astype(values.dtype)
    return (tiled * flags[:, None, :, None]).reshape(height, breadth)


def whole_slab(a_tiles, a_occupancy, b_tiles, b_occupancy):
    a_kept = keep_blocks(a_tiles, a_occupancy)
    b_kept = keep_blocks(b_tiles, b_occupancy)
    partial_value = jnp.dot(
        lax.all_gather(a_kept, "col", axis=1, tiled=True),
        lax.all_gather(b_kept, "row", axis=0, tiled=True),
        preferred_element_type=jnp.float32,
    )
    return lax.psum_scatter(partial_value, "layer", scatter_dimension=0, tiled=True)


def slots_for(blocks, spread):
    if blocks < 16:
        return blocks + 1
    room = (blocks * 7 + 15) // 16 + int(round(spread * blocks**0.5))
    return min(blocks, room) + 1


def cuts_for(stages, spread):
    cuts, blocks = [0], 0
    for stage in stages:
        blocks += stage.rows * stage.wide
        cuts.append(max(slots_for(blocks, spread), cuts[-1] + 1))
    return cuts


class Stage(typing.NamedTuple):
    row: int
    rows: int
    first: int
    wide: int


def header_of(occupancy):
    rows, columns = occupancy.shape
    flags = occupancy.astype(jnp.bfloat16)
    return jnp.pad(flags, ((0, BLOCK - rows), (0, BLOCK - columns)))


def mark_row(i):
    return BLOCK - 16 * (i + 1)


def pack_kernel(place, stages, ends, cuts, other, turn_ref, flags_ref, other_ref, header_ref, values_ref, *refs):
    parts, (over_out, held, sem, out_sems) = refs[: len(cuts) - 1], refs[-4:]
    header = pltpu.make_async_copy(header_ref, held.at[0], sem)
    header.start()

    def step_of(stage):
        def step(u, slot):
            row, column = place(stage, u, turn_ref[0])
            flag = flags_ref[row, column]

            @pl.when(flag > 0)
            def _():
                pltpu.make_async_copy(
                    values_ref.at[
                        pl.ds(pl.multiple_of(row * BLOCK, BLOCK), BLOCK),
                        pl.ds(pl.multiple_of(column * BLOCK, BLOCK), BLOCK),
                    ],
                    held.at[jnp.minimum(slot, cuts[-1])],
                    sem,
                ).start()

            return slot + flag

        return step

    slot, over, marks = jnp.int32(1), jnp.int32(0), []
    for stage, cut in zip(stages, ends[1:]):
        marks.append(slot)
        slot = lax.fori_loop(0, stage.rows * stage.wide, step_of(stage), slot, unroll=4)
        over = jnp.maximum(over, jnp.where(slot > cut, 1, 0))
    if other is not None:
        other_place, other_stages, other_ends = other
        spent = jnp.int32(1)
        for stage, cut in zip(other_stages, other_ends[1:]):

            def count(u, spent):
                row, column = other_place(stage, u, turn_ref[0])
                return spent + other_ref[row, column]

            spent = lax.fori_loop(0, stage.rows * stage.wide, count, spent, unroll=16)
            over = jnp.maximum(over, jnp.where(spent > cut, 1, 0))

    def settle(t, _):
        header.wait()
        return 0

    lax.fori_loop(0, slot, settle, 0)
    for i, mark in enumerate([over, *marks]):
        row = mark_row(i)
        held[0, row : row + 16, :] = jnp.full((16, BLOCK), mark.astype(jnp.float32)).astype(held.dtype)
    over_out[0] = over
    copies = [
        pltpu.make_async_copy(held.at[pl.ds(lo, hi - lo)], part, out_sems.at[i])
        for i, (part, lo, hi) in enumerate(zip(parts, cuts[:-1], cuts[1:]))
    ]
    for copy in copies:
        copy.start()
    for copy in copies:
        copy.wait()


def pack(values, occupancy, turn, place, stages, ends, cuts, other_flags, other):
    *parts, done = pl.pallas_call(
        functools.partial(pack_kernel, place, stages, ends, cuts, other),
        grid_spec=pltpu.PrefetchScalarGridSpec(
            num_scalar_prefetch=3,
            grid=(),
            in_specs=[pl.BlockSpec(memory_space=pl.ANY)] * 2,
            out_specs=[pl.BlockSpec(memory_space=pl.ANY)] * (len(cuts) - 1)
            + [pl.BlockSpec(memory_space=pltpu.SMEM)],
            scratch_shapes=[
                pltpu.VMEM((cuts[-1] + 1, BLOCK, BLOCK), values.dtype),
                pltpu.SemaphoreType.DMA,
                pltpu.SemaphoreType.DMA((len(cuts) - 1,)),
            ],
        ),
        out_shape=[
            jax.ShapeDtypeStruct((hi - lo, BLOCK, BLOCK), values.dtype) for lo, hi in zip(cuts[:-1], cuts[1:])
        ]
        + [jax.ShapeDtypeStruct((1,), jnp.int32)],
        compiler_params=pltpu.CompilerParams(vmem_limit_bytes=VMEM_LIMIT),
        cost_estimate=SMALL,
        name="pack",
    )(turn, occupancy, other_flags, header_of(occupancy), values)
    return parts, done


def load_list(parts, cuts, held, sems):
    return [
        pltpu.make_async_copy(part, held.at[pl.ds(lo, hi - lo)], sems.at[i])
        for i, (part, lo, hi) in enumerate(zip(parts, cuts[:-1], cuts[1:]))
    ]


def unpack_b_kernel(k_blocks, first, stop, cuts, shard_ref, flags_ref, *refs):
    parts, (out_ref, done_ref, held, sems, sem) = refs[: len(cuts) - 1], refs[-5:]
    done_ref[0] = 0
    nothing = cuts[-1]
    copies = load_list(parts, cuts, held, sems)
    for copy in copies:
        copy.start()
    held[nothing] = jnp.zeros_like(held[nothing])

    def flag_of(t):
        return flags_ref[t % k_blocks, t // k_blocks]

    slot = lax.fori_loop(0, first * k_blocks, lambda t, slot: slot + flag_of(t), jnp.int32(1), unroll=8)
    for copy in copies:
        copy.wait()
    base = shard_ref[0] * k_blocks

    def step(t, slot):
        flag = flag_of(first * k_blocks + t)
        pltpu.make_async_copy(
            held.at[jnp.where(flag > 0, jnp.minimum(slot, nothing), nothing)],
            out_ref.at[
                pl.ds(pl.multiple_of((base + t % k_blocks) * BLOCK, BLOCK), BLOCK),
                pl.ds(pl.multiple_of(t // k_blocks * BLOCK, BLOCK), BLOCK),
            ],
            sem,
        ).start()
        return slot + flag

    lax.fori_loop(0, (stop - first) * k_blocks, step, slot, unroll=8)
    written = out_ref.at[pl.ds(pl.multiple_of(base * BLOCK, BLOCK), k_blocks * BLOCK)]
    pltpu.make_async_copy(written, written, sem).wait()


def unpack_b(parts, flags, shard, shards, first, stop, k_blocks, cuts, into):
    n = len(parts)
    operands = [*parts] + ([] if into is None else [into])
    return pl.pallas_call(
        functools.partial(unpack_b_kernel, k_blocks, first, stop, cuts),
        grid_spec=pltpu.PrefetchScalarGridSpec(
            num_scalar_prefetch=2,
            grid=(),
            in_specs=[pl.BlockSpec(memory_space=pl.ANY)] * len(operands),
            out_specs=[pl.BlockSpec(memory_space=pl.ANY), pl.BlockSpec(memory_space=pltpu.SMEM)],
            scratch_shapes=[
                pltpu.VMEM((cuts[-1] + 1, BLOCK, BLOCK), parts[0].dtype),
                pltpu.SemaphoreType.DMA((n,)),
                pltpu.SemaphoreType.DMA,
            ],
        ),
        out_shape=[
            jax.ShapeDtypeStruct((shards * k_blocks * BLOCK, (stop - first) * BLOCK), parts[0].dtype),
            jax.ShapeDtypeStruct((1,), jnp.int32),
        ],
        input_output_aliases={} if into is None else {2 + n: 0},
        compiler_params=pltpu.CompilerParams(vmem_limit_bytes=VMEM_LIMIT),
        cost_estimate=SMALL,
        name="unpack_b",
    )(shard, flags, *operands)


def multiply_kernel(plan, turn_ref, column_ref, flags_ref, marks_ref, *refs):
    place, stages, blocks, cuts, shards, halves, given, carried, final, starts, ends = plan
    stage = stages[-1]
    rows, wide = stage.rows, stage.wide
    n = len(cuts) - 2
    gathered_ref, refs = refs[0], refs[1:]
    lists = [refs[s * n : (s + 1) * n] for s in range(shards)]
    refs = refs[shards * n :]
    b_refs, refs = refs[:halves], refs[halves:]
    codes_in, refs = refs[: 2 * halves * given], refs[2 * halves * given :]
    before, refs = refs[:carried], refs[carried:]
    outs, (dense, sem, total) = refs[:-3], refs[-3:]
    turn = turn_ref[0]

    def fill():
        dense[...] = jnp.zeros_like(dense)
        started = jnp.int32(0)
        for s in range(shards):
            column = column_ref[s]
            parts = [gathered_ref.at[column], *lists[s]]

            def flag_of(stage, u):
                row, k = place(stage, u, turn)
                return flags_ref[column * blocks + row, k]

            def step(u, slot):
                flag = flag_of(stage, u)
                target = dense.at[
                    pl.ds(pl.multiple_of(u // wide * BLOCK, BLOCK), BLOCK),
                    pl.ds(pl.multiple_of((column * wide + u % wide) * BLOCK, BLOCK), BLOCK),
                ]
                for part, lo, hi in zip(parts, cuts[:-1], cuts[1:]):

                    @pl.when((flag > 0) & (slot >= lo) & (slot < hi))
                    def _():
                        pltpu.make_async_copy(part.at[slot - lo], target, sem).start()

                return slot + flag

            slot = marks_ref[column, mark_row(len(stages))]
            end = lax.fori_loop(0, rows * wide, step, slot, unroll=4)
            started += jnp.minimum(end, cuts[-1]) - jnp.minimum(slot, cuts[-1])

        def settle(t, _):
            pltpu.make_async_copy(gathered_ref.at[0, 0], dense.at[:BLOCK, :BLOCK], sem).wait()
            return 0

        lax.fori_loop(0, started, settle, 0)

    pl.when(pl.program_id(0) == 0)(fill)

    def finish(value, h):
        if not final:
            codes_ref, factors_ref = outs
            for r in range(rows):
                span = slice(r * BLOCK, (r + 1) * BLOCK)
                top = jnp.max(jnp.abs(value[span]), axis=0, keepdims=True)
                factor = jnp.where(top > 0, 32767.0 / top, 0.0)
                codes_ref[span] = jnp.round(value[span] * factor).astype(jnp.int32).astype(jnp.int16)
                factors_ref[r] = top * (1.0 / 32767.0)
            return
        (out_ref,) = outs
        for r in range(rows):
            span = slice(r * BLOCK, (r + 1) * BLOCK)
            some = value[span]
            for q in range(given):
                codes, factors = codes_in[2 * (q * halves + h) : 2 * (q * halves + h) + 2]
                some += codes[span].astype(jnp.int32).astype(jnp.float32) * factors[r]
            for earlier in before:
                some += earlier[span]
            out_ref[span] = some

    for h, b_ref in enumerate(b_refs):

        @pl.when((pl.program_id(0) >= starts[h]) & (pl.program_id(0) < ends[h]))
        def _():
            b_here = b_ref[...].reshape(-1, b_ref.shape[-1])
            total[...] = jnp.dot(dense[...], b_here, preferred_element_type=jnp.float32)
            finish(total, h)


def multiply(gathered, lists, flags, marks, turn, columns, place, stages, k_blocks, cuts, b_halves, final, cost, received=(), before=()):
    shards, halves = len(lists), len(b_halves)
    stage = stages[-1]
    n = len(cuts) - 2
    widths = [b_half.shape[1] for b_half in b_halves]
    shared = math.gcd(*widths)
    tile = max(t for t in (BLOCK, 256, 512) if shared % t == 0 and t * stage.wide <= TILE_ROOM)
    ends = [sum(widths[: h + 1]) // tile for h in range(halves)]
    starts = [0] + ends[:-1]
    deep = math.gcd(math.gcd(stage.first, stage.wide), k_blocks)
    layers, skip = stage.wide // deep, stage.first // deep
    assert skip % layers == 0
    tall = stage.rows * BLOCK
    whole = pl.BlockSpec(memory_space=pl.ANY)

    def at(h, *fixed):
        return lambda j, *_: (*fixed, jnp.clip(j - starts[h], 0, ends[h] - starts[h] - 1))

    in_specs = [whole] * (1 + shards * n)
    operands = [gathered] + [p for parts in lists for p in parts[:n]]
    for h, b_half in enumerate(b_halves):
        in_specs.append(pl.BlockSpec((shards, layers, deep * BLOCK, tile), at(h, 0, skip // layers, 0)))
        operands.append(b_half.reshape(shards, k_blocks // deep, deep * BLOCK, widths[h]))
    for pairs in received:
        for h, (codes, factors) in enumerate(pairs):
            in_specs.append(pl.BlockSpec((tall, tile), at(h, 0)))
            in_specs.append(pl.BlockSpec((stage.rows, 1, tile), at(h, 0, 0)))
            operands += [codes, factors]
    in_specs += [pl.BlockSpec((tall, tile), lambda j, *_: (0, j))] * len(before)
    operands += [*before]
    out_specs = [pl.BlockSpec((tall, tile), lambda j, *_: (0, j))]
    if final:
        out_shape = [jax.ShapeDtypeStruct((tall, sum(widths)), jnp.float32)]
    else:
        out_specs.append(pl.BlockSpec((stage.rows, 1, tile), lambda j, *_: (0, 0, j)))
        out_shape = [
            jax.ShapeDtypeStruct((tall, sum(widths)), jnp.int16),
            jax.ShapeDtypeStruct((stage.rows, 1, sum(widths)), jnp.float32),
        ]
    blocks = flags.shape[0] // shards
    plan = (place, stages, blocks, cuts, shards, halves, len(received), len(before), final, starts, ends)
    return pl.pallas_call(
        functools.partial(multiply_kernel, plan),
        grid_spec=pltpu.PrefetchScalarGridSpec(
            num_scalar_prefetch=4,
            grid=(ends[-1],),
            in_specs=in_specs,
            out_specs=out_specs,
            scratch_shapes=[
                pltpu.VMEM((tall, shards * stage.wide * BLOCK), b_halves[0].dtype),
                pltpu.SemaphoreType.DMA,
                pltpu.VMEM((tall, tile), jnp.float32),
            ],
        ),
        out_shape=out_shape,
        compiler_params=pltpu.CompilerParams(vmem_limit_bytes=VMEM_LIMIT),
        cost_estimate=cost,
        name="multiply",
    )(turn, columns, flags, marks, *operands)


def largest_over(value, axis, size, step=1, stop=None):
    while step < (stop or size):
        value = jnp.maximum(value, lax.ppermute(value, axis, [(i, i ^ step) for i in range(size)]))
        step *= 2
    return value


def after(value, *others):
    return lax.optimization_barrier((value, *others))[0]


def per_device(sizes, a_tiles, a_occupancy, b_tiles, b_occupancy):
    rows, cols, layers = sizes
    me_row, me_col, me_layer = (lax.axis_index(axis).astype(jnp.int32) for axis in ("row", "col", "layer"))
    a_rows, a_k = a_occupancy.shape
    b_k, b_columns = b_occupancy.shape
    piece = a_rows // layers
    given = a_rows - piece
    turn = me_layer.reshape(1)

    def a_place(stage, u, layer):
        row, k = stage.row + u // stage.wide, stage.first + u % stage.wide
        return lax.rem(row + (layer + 1) * piece, a_rows), k

    def b_place(stage, u, _):
        return stage.first + u % stage.wide, stage.row + u // stage.wide

    early = a_k * 3 // 4
    a_stages = [
        stage
        for stage in (
            Stage(0, given, 0, a_k),
            Stage(given, piece, 0, early),
            Stage(given, piece, early, a_k - early),
        )
        if stage.rows * stage.wide
    ]
    half = b_columns * 5 // 8
    b_stages = [Stage(0, half, 0, b_k), Stage(half, b_columns - half, 0, b_k)]
    a_cuts, b_ends = cuts_for(a_stages, 1.77), cuts_for(b_stages, 2.0)
    b_cuts = sorted({*b_ends, (b_ends[1] + b_ends[2] + 1) // 2})
    b_counts = [b_cuts.index(end) for end in b_ends[1:]]

    a_parts, done = pack(
        a_tiles, a_occupancy, turn, a_place, a_stages, a_cuts, a_cuts, b_occupancy, (b_place, b_stages, b_ends)
    )
    gathered = lax.all_gather(a_parts[0], "col", axis=0)
    b_parts, done = pack(
        b_tiles, b_occupancy, after(turn, done), b_place, b_stages, b_ends, b_cuts, b_occupancy, None
    )

    pair = 2 if rows % 2 == 0 else 1
    swap = [(r, r ^ 1) for r in range(rows)]
    b_dense = [None] * len(b_stages)

    def unpack(h, shard, lists, done):
        stage = b_stages[h]
        flags = lists[0][0, :b_k, :b_columns].astype(jnp.int32)
        b_dense[h], done = unpack_b(
            lists[: b_counts[h]], flags, after(shard.reshape(1), done), rows, stage.row, stage.row + stage.rows, b_k,
            b_cuts[: b_counts[h] + 1], b_dense[h],
        )
        return done

    def across(part, hop):
        return lax.ppermute(part, "row", [(r, (r + pair * hop) % rows) for r in range(rows)])

    hops = range(1, rows // pair)
    shards = [lax.rem(me_row - pair * hop + rows, rows) for hop in range(rows // pair)]
    came = {(0, hop): across(b_parts[0], hop) for hop in hops}
    lists = {0: b_parts}
    if pair == 2:
        lists[1] = [lax.ppermute(part, "row", swap) for part in b_parts]
    for side in range(pair):
        for h in range(len(b_stages)):
            done = unpack(h, shards[0] ^ side, lists[side], done)
    sides = {}
    for hop in hops:
        here = after(came[0, hop], done)
        sides[hop] = [[here], [lax.ppermute(here, "row", swap)]][:pair]
        for i in range(1, len(b_parts)):
            came[i, hop] = across(after(b_parts[i], here), hop)
    for side in range(pair):
        for hop in hops:
            done = unpack(0, shards[hop] ^ side, sides[hop][side], done)

    a_lists = [[] for _ in range(cols)]
    waits = [done] * cols
    for part in a_parts[1:]:
        a_lists[0].append(part)
        for hop in range(1, cols):
            there = [(c, (c + hop) % cols) for c in range(cols)]
            waits[hop] = lax.ppermute(after(part, waits[hop], gathered), "col", there)
            a_lists[hop].append(waits[hop])
    a_columns = lax.rem(me_col - jnp.arange(cols, dtype=jnp.int32) + cols, cols)
    a_flags = gathered[:, 0, :a_rows, :a_k].astype(jnp.int32).reshape(cols * a_rows, a_k)

    a_marks = gathered[:, 0, :, 0].astype(jnp.int32)

    def product_of(g, halves, done, **more):
        return multiply(
            gathered, a_lists, a_flags, a_marks, after(turn, done), a_columns, a_place, a_stages[: g + 1], a_k, a_cuts[: g + 2],
            halves, **more
        )

    over = jnp.max(gathered[:, 0, mark_row(0) : mark_row(0) + 8].astype(jnp.float32), axis=0)
    over = largest_over(over, "layer", layers)

    received = [[] for _ in range(layers - 1)]
    for h in range(len(b_stages)):
        if h:
            for hop in hops:
                here = [after(came[i, hop], done) for i in range(1, b_counts[h])]
                there = [lax.ppermute(part, "row", swap) for part in here]
                for side, more in zip(range(pair), (here, there)):
                    done = unpack(h, shards[hop] ^ side, sides[hop][side] + more, done)
        codes, factors = product_of(0, [b_dense[h]], done, final=False, cost=SMALL if h else LARGE)
        done = factors
        over = largest_over(after(over, done), "row", rows, 1 << h, 2 << h if h + 1 < len(b_stages) else rows)
        for q in range(layers - 1):
            there = [(i, (i + 1 + q) % layers) for i in range(layers)]
            own = codes[q * piece * BLOCK : (q + 1) * piece * BLOCK], factors[q * piece : (q + 1) * piece]
            received[q].append(tuple(lax.ppermute(x, "layer", there) for x in own))

    (product,) = product_of(1, b_dense, done, final=True, cost=LARGE)
    for g in range(2, len(a_stages)):
        last = g == len(a_stages) - 1
        (product,) = product_of(
            g, b_dense, done, final=True, cost=SMALL, received=received if last else (), before=(product,)
        )
    return lax.cond(
        over[0, 0] > 0,
        lambda: whole_slab(a_tiles, a_occupancy, b_tiles, b_occupancy),
        lambda: product,
    )


def solution(mesh):
    sizes = tuple(mesh.shape[axis] for axis in ("row", "col", "layer"))
    in_specs = (
        P("row", ("layer", "col")),
        P("row", ("layer", "col")),
        P(("layer", "row"), "col"),
        P(("layer", "row"), "col"),
    )
    out_specs = P(("row", "layer"), "col")
    return jax.shard_map(
        functools.partial(per_device, sizes), mesh=mesh, in_specs=in_specs, out_specs=out_specs, check_vma=False
    )
```

```python
import functools
import math
import typing

import jax
import jax.numpy as jnp
from jax import lax
from jax.experimental import pallas as pl
from jax.experimental.pallas import tpu as pltpu
from jax.sharding import PartitionSpec as P

BLOCK = 128
VMEM_LIMIT = 56 * 1024 * 1024
TILE_ROOM = 256 * 16
SMALL = pl.CostEstimate(flops=1, bytes_accessed=1, transcendentals=0)
LARGE = pl.CostEstimate(flops=10**12, bytes_accessed=1, transcendentals=0)


def keep_blocks(values, occupancy):
    height, breadth = values.shape
    tiled = values.reshape(height // BLOCK, BLOCK, breadth // BLOCK, BLOCK)
    flags = occupancy.astype(values.dtype)
    return (tiled * flags[:, None, :, None]).reshape(height, breadth)


def whole_slab(a_tiles, a_occupancy, b_tiles, b_occupancy):
    a_kept = keep_blocks(a_tiles, a_occupancy)
    b_kept = keep_blocks(b_tiles, b_occupancy)
    partial_value = jnp.dot(
        lax.all_gather(a_kept, "col", axis=1, tiled=True),
        lax.all_gather(b_kept, "row", axis=0, tiled=True),
        preferred_element_type=jnp.float32,
    )
    return lax.psum_scatter(partial_value, "layer", scatter_dimension=0, tiled=True)


def slots_for(blocks, spread):
    if blocks < 16:
        return blocks + 1
    room = (blocks * 7 + 15) // 16 + int(round(spread * blocks**0.5))
    return min(blocks, room) + 1


def cuts_for(stages, spread):
    cuts, blocks = [0], 0
    for stage in stages:
        blocks += stage.rows * stage.wide
        cuts.append(max(slots_for(blocks, spread), cuts[-1] + 1))
    return cuts


class Stage(typing.NamedTuple):
    row: int
    rows: int
    first: int
    wide: int


def header_of(occupancy):
    rows, columns = occupancy.shape
    flags = occupancy.astype(jnp.bfloat16)
    return jnp.pad(flags, ((0, BLOCK - rows), (0, BLOCK - columns)))


def mark_row(i):
    return BLOCK - 16 * (i + 1)


def pack_kernel(place, stages, ends, cuts, other, turn_ref, flags_ref, other_ref, header_ref, values_ref, *refs):
    parts, (over_out, held, sem, out_sems) = refs[: len(cuts) - 1], refs[-4:]
    header = pltpu.make_async_copy(header_ref, held.at[0], sem)
    header.start()

    def step_of(stage):
        def step(u, slot):
            row, column = place(stage, u, turn_ref[0])
            flag = flags_ref[row, column]

            @pl.when(flag > 0)
            def _():
                pltpu.make_async_copy(
                    values_ref.at[
                        pl.ds(pl.multiple_of(row * BLOCK, BLOCK), BLOCK),
                        pl.ds(pl.multiple_of(column * BLOCK, BLOCK), BLOCK),
                    ],
                    held.at[jnp.minimum(slot, cuts[-1])],
                    sem,
                ).start()

            return slot + flag

        return step

    slot, over, marks = jnp.int32(1), jnp.int32(0), []
    for stage, cut in zip(stages, ends[1:]):
        marks.append(slot)
        slot = lax.fori_loop(0, stage.rows * stage.wide, step_of(stage), slot, unroll=4)
        over = jnp.maximum(over, jnp.where(slot > cut, 1, 0))
    if other is not None:
        other_place, other_stages, other_ends = other
        spent = jnp.int32(1)
        for stage, cut in zip(other_stages, other_ends[1:]):

            def count(u, spent):
                row, column = other_place(stage, u, turn_ref[0])
                return spent + other_ref[row, column]

            spent = lax.fori_loop(0, stage.rows * stage.wide, count, spent, unroll=16)
            over = jnp.maximum(over, jnp.where(spent > cut, 1, 0))

    def settle(t, _):
        header.wait()
        return 0

    lax.fori_loop(0, slot, settle, 0)
    for i, mark in enumerate([over, *marks]):
        row = mark_row(i)
        held[0, row : row + 16, :] = jnp.full((16, BLOCK), mark.astype(jnp.float32)).astype(held.dtype)
    over_out[0] = over
    copies = [
        pltpu.make_async_copy(held.at[pl.ds(lo, hi - lo)], part, out_sems.at[i])
        for i, (part, lo, hi) in enumerate(zip(parts, cuts[:-1], cuts[1:]))
    ]
    for copy in copies:
        copy.start()
    for copy in copies:
        copy.wait()


def pack(values, occupancy, turn, place, stages, ends, cuts, other_flags, other):
    *parts, done = pl.pallas_call(
        functools.partial(pack_kernel, place, stages, ends, cuts, other),
        grid_spec=pltpu.PrefetchScalarGridSpec(
            num_scalar_prefetch=3,
            grid=(),
            in_specs=[pl.BlockSpec(memory_space=pl.ANY)] * 2,
            out_specs=[pl.BlockSpec(memory_space=pl.ANY)] * (len(cuts) - 1)
            + [pl.BlockSpec(memory_space=pltpu.SMEM)],
            scratch_shapes=[
                pltpu.VMEM((cuts[-1] + 1, BLOCK, BLOCK), values.dtype),
                pltpu.SemaphoreType.DMA,
                pltpu.SemaphoreType.DMA((len(cuts) - 1,)),
            ],
        ),
        out_shape=[
            jax.ShapeDtypeStruct((hi - lo, BLOCK, BLOCK), values.dtype) for lo, hi in zip(cuts[:-1], cuts[1:])
        ]
        + [jax.ShapeDtypeStruct((1,), jnp.int32)],
        compiler_params=pltpu.CompilerParams(vmem_limit_bytes=VMEM_LIMIT),
        cost_estimate=SMALL,
        name="pack",
    )(turn, occupancy, other_flags, header_of(occupancy), values)
    return parts, done


def load_list(parts, cuts, held, sems):
    return [
        pltpu.make_async_copy(part, held.at[pl.ds(lo, hi - lo)], sems.at[i])
        for i, (part, lo, hi) in enumerate(zip(parts, cuts[:-1], cuts[1:]))
    ]


def unpack_b_kernel(k_blocks, first, stop, cuts, shard_ref, flags_ref, *refs):
    parts, (out_ref, done_ref, held, sems, sem) = refs[: len(cuts) - 1], refs[-5:]
    done_ref[0] = 0
    nothing = cuts[-1]
    copies = load_list(parts, cuts, held, sems)
    for copy in copies:
        copy.start()
    held[nothing] = jnp.zeros_like(held[nothing])

    def flag_of(t):
        return flags_ref[t % k_blocks, t // k_blocks]

    slot = lax.fori_loop(0, first * k_blocks, lambda t, slot: slot + flag_of(t), jnp.int32(1), unroll=8)
    for copy in copies:
        copy.wait()
    base = shard_ref[0] * k_blocks

    def step(t, slot):
        flag = flag_of(first * k_blocks + t)
        pltpu.make_async_copy(
            held.at[jnp.where(flag > 0, jnp.minimum(slot, nothing), nothing)],
            out_ref.at[
                pl.ds(pl.multiple_of((base + t % k_blocks) * BLOCK, BLOCK), BLOCK),
                pl.ds(pl.multiple_of(t // k_blocks * BLOCK, BLOCK), BLOCK),
            ],
            sem,
        ).start()
        return slot + flag

    lax.fori_loop(0, (stop - first) * k_blocks, step, slot, unroll=8)
    written = out_ref.at[pl.ds(pl.multiple_of(base * BLOCK, BLOCK), k_blocks * BLOCK)]
    pltpu.make_async_copy(written, written, sem).wait()


def unpack_b(parts, flags, shard, shards, first, stop, k_blocks, cuts, into):
    n = len(parts)
    operands = [*parts] + ([] if into is None else [into])
    return pl.pallas_call(
        functools.partial(unpack_b_kernel, k_blocks, first, stop, cuts),
        grid_spec=pltpu.PrefetchScalarGridSpec(
            num_scalar_prefetch=2,
            grid=(),
            in_specs=[pl.BlockSpec(memory_space=pl.ANY)] * len(operands),
            out_specs=[pl.BlockSpec(memory_space=pl.ANY), pl.BlockSpec(memory_space=pltpu.SMEM)],
            scratch_shapes=[
                pltpu.VMEM((cuts[-1] + 1, BLOCK, BLOCK), parts[0].dtype),
                pltpu.SemaphoreType.DMA((n,)),
                pltpu.SemaphoreType.DMA,
            ],
        ),
        out_shape=[
            jax.ShapeDtypeStruct((shards * k_blocks * BLOCK, (stop - first) * BLOCK), parts[0].dtype),
            jax.ShapeDtypeStruct((1,), jnp.int32),
        ],
        input_output_aliases={} if into is None else {2 + n: 0},
        compiler_params=pltpu.CompilerParams(vmem_limit_bytes=VMEM_LIMIT),
        cost_estimate=SMALL,
        name="unpack_b",
    )(shard, flags, *operands)


def multiply_kernel(plan, turn_ref, column_ref, flags_ref, marks_ref, *refs):
    place, stages, blocks, cuts, shards, halves, given, carried, pieces, starts, ends = plan
    stage = stages[-1]
    rows, wide = stage.rows, stage.wide
    n = len(cuts) - 1
    gathered_refs, refs = refs[:n], refs[n:]
    b_refs, refs = refs[:halves], refs[halves:]
    codes_in, refs = refs[: halves * given], refs[halves * given :]
    before, refs = refs[:carried], refs[carried:]
    over_ref, out_ref, dense, sem, total = refs[-5:]
    turn = turn_ref[0]

    def fill():
        dense[...] = jnp.zeros_like(dense)
        started = jnp.int32(0)
        for s in range(shards):
            column = column_ref[s]
            parts = [ref.at[column] for ref in gathered_refs]

            def flag_of(stage, u):
                row, k = place(stage, u, turn)
                return flags_ref[column * blocks + row, k]

            def step(u, slot):
                flag = flag_of(stage, u)
                target = dense.at[
                    pl.ds(pl.multiple_of(u // wide * BLOCK, BLOCK), BLOCK),
                    pl.ds(pl.multiple_of((column * wide + u % wide) * BLOCK, BLOCK), BLOCK),
                ]
                for part, lo, hi in zip(parts, cuts[:-1], cuts[1:]):

                    @pl.when((flag > 0) & (slot >= lo) & (slot < hi))
                    def _():
                        pltpu.make_async_copy(part.at[slot - lo], target, sem).start()

                return slot + flag

            slot = marks_ref[column, mark_row(len(stages))]
            end = lax.fori_loop(0, rows * wide, step, slot, unroll=4)
            started += jnp.minimum(end, cuts[-1]) - jnp.minimum(slot, cuts[-1])

        def settle(t, _):
            pltpu.make_async_copy(gathered_refs[0].at[0, 0], dense.at[:BLOCK, :BLOCK], sem).wait()
            return 0

        lax.fori_loop(0, started, settle, 0)

    pl.when(pl.program_id(0) == 0)(fill)

    def code(value):
        share = rows // pieces
        for q in range(pieces):
            base = q * (share * BLOCK + 16)
            powers = []
            for r in range(share):
                some = value[(q * share + r) * BLOCK : (q * share + r + 1) * BLOCK]
                top = jnp.max(jnp.abs(some), axis=0, keepdims=True)
                power = jnp.clip(jnp.ceil(jnp.log2(top)), -60.0, 60.0)
                some = jnp.clip(jnp.round(some * jnp.exp2(15.0 - power)), -32767.0, 32767.0)
                out_ref[base + r * BLOCK : base + (r + 1) * BLOCK] = some.astype(jnp.int32).astype(jnp.int16)
                powers.append(power)
            flag = jnp.broadcast_to(over_ref[0:1, 0:1], powers[0].shape)
            notes = jnp.concatenate(powers + [flag] * (16 - share), axis=0)
            out_ref[base + share * BLOCK : base + share * BLOCK + 16] = notes.astype(jnp.int32).astype(jnp.int16)

    def finish(value, h):
        for r in range(rows):
            span = slice(r * BLOCK, (r + 1) * BLOCK)
            some = value[span]
            for q in range(given):
                codes = codes_in[q * halves + h]
                notes = codes[rows * BLOCK : rows * BLOCK + 16].astype(jnp.int32).astype(jnp.float32)
                some += codes[span].astype(jnp.int32).astype(jnp.float32) * jnp.exp2(notes[r : r + 1] - 15.0)
            for earlier in before:
                some += earlier[span]
            out_ref[span] = some

    for h, b_ref in enumerate(b_refs):

        @pl.when((pl.program_id(0) >= starts[h]) & (pl.program_id(0) < ends[h]))
        def _():
            b_here = b_ref[...].reshape(-1, b_ref.shape[-1])
            total[...] = jnp.dot(dense[...], b_here, preferred_element_type=jnp.float32)
            if pieces:
                code(total)
            else:
                finish(total, h)


def multiply(parts, flags, marks, turn, columns, place, stages, k_blocks, cuts, b_halves, over, pieces=0, received=(), before=()):
    shards, halves = parts[0].shape[0], len(b_halves)
    stage = stages[-1]
    n = len(cuts) - 1
    widths = [b_half.shape[1] for b_half in b_halves]
    shared = math.gcd(*widths)
    tile = max(t for t in (BLOCK, 256, 512) if shared % t == 0 and t * stage.wide <= TILE_ROOM)
    ends = [sum(widths[: h + 1]) // tile for h in range(halves)]
    starts = [0] + ends[:-1]
    deep = math.gcd(math.gcd(stage.first, stage.wide), k_blocks)
    layers, skip = stage.wide // deep, stage.first // deep
    assert skip % layers == 0
    tall = stage.rows * BLOCK
    whole = pl.BlockSpec(memory_space=pl.ANY)

    def at(h, *fixed):
        return lambda j, *_: (*fixed, jnp.clip(j - starts[h], 0, ends[h] - starts[h] - 1))

    in_specs = [whole] * n
    operands = [*parts[:n]]
    for h, b_half in enumerate(b_halves):
        in_specs.append(pl.BlockSpec((shards, layers, deep * BLOCK, tile), at(h, 0, skip // layers, 0)))
        operands.append(b_half.reshape(shards, k_blocks // deep, deep * BLOCK, widths[h]))
    for pairs in received:
        for h, codes in enumerate(pairs):
            in_specs.append(pl.BlockSpec((tall + 16, tile), at(h, 0)))
            operands.append(codes)
    in_specs += [pl.BlockSpec((tall, tile), lambda j, *_: (0, j))] * len(before)
    operands += [*before]
    in_specs.append(pl.BlockSpec(memory_space=pltpu.VMEM))
    operands.append(over)
    high = tall + 16 * pieces
    plan = (place, stages, flags.shape[0] // shards, cuts, shards, halves, len(received), len(before), pieces, starts, ends)
    return pl.pallas_call(
        functools.partial(multiply_kernel, plan),
        grid_spec=pltpu.PrefetchScalarGridSpec(
            num_scalar_prefetch=4,
            grid=(ends[-1],),
            in_specs=in_specs,
            out_specs=pl.BlockSpec((high, tile), lambda j, *_: (0, j)),
            scratch_shapes=[
                pltpu.VMEM((tall, shards * stage.wide * BLOCK), b_halves[0].dtype),
                pltpu.SemaphoreType.DMA,
                pltpu.VMEM((tall, tile), jnp.float32),
            ],
        ),
        out_shape=jax.ShapeDtypeStruct((high, sum(widths)), jnp.int16 if pieces else jnp.float32),
        compiler_params=pltpu.CompilerParams(vmem_limit_bytes=VMEM_LIMIT),
        cost_estimate=SMALL,
        name="multiply",
    )(turn, columns, flags, marks, *operands)


def largest_over(value, axis, size, step=1, stop=None):
    while step < (stop or size):
        value = jnp.maximum(value, lax.ppermute(value, axis, [(i, i ^ step) for i in range(size)]))
        step *= 2
    return value


def after(value, *others):
    return lax.optimization_barrier((value, *others))[0]


def per_device(sizes, a_tiles, a_occupancy, b_tiles, b_occupancy):
    rows, cols, layers = sizes
    me_row, me_col, me_layer = (lax.axis_index(axis).astype(jnp.int32) for axis in ("row", "col", "layer"))
    a_rows, a_k = a_occupancy.shape
    b_k, b_columns = b_occupancy.shape
    piece = a_rows // layers
    given = a_rows - piece
    turn = me_layer.reshape(1)

    def a_place(stage, u, layer):
        row, k = stage.row + u // stage.wide, stage.first + u % stage.wide
        return lax.rem(row + (layer + 1) * piece, a_rows), k

    def b_place(stage, u, _):
        return stage.first + u % stage.wide, stage.row + u // stage.wide

    early = a_k * 3 // 4
    a_stages = [
        stage
        for stage in (
            Stage(0, given, 0, a_k),
            Stage(given, piece, 0, early),
            Stage(given, piece, early, a_k - early),
        )
        if stage.rows * stage.wide
    ]
    half = b_columns * 5 // 8
    b_stages = [Stage(0, half, 0, b_k), Stage(half, b_columns - half, 0, b_k)]
    a_cuts, b_ends = cuts_for(a_stages, 1.77), cuts_for(b_stages, 2.0)
    b_cuts = sorted({*b_ends, (b_ends[1] + b_ends[2] + 1) // 2})
    b_counts = [b_cuts.index(end) for end in b_ends[1:]]

    a_parts, done = pack(
        a_tiles, a_occupancy, turn, a_place, a_stages, a_cuts, a_cuts, b_occupancy, (b_place, b_stages, b_ends)
    )
    joint = [lax.all_gather(part, "col", axis=0) for part in a_parts]
    gathered = joint[0]
    b_parts, done = pack(
        b_tiles, b_occupancy, after(turn, done), b_place, b_stages, b_ends, b_cuts, b_occupancy, None
    )

    pair = 2 if rows % 2 == 0 else 1
    swap = [(r, r ^ 1) for r in range(rows)]
    b_dense = [None] * len(b_stages)

    def unpack(h, shard, lists, done):
        stage = b_stages[h]
        flags = lists[0][0, :b_k, :b_columns].astype(jnp.int32)
        b_dense[h], done = unpack_b(
            lists[: b_counts[h]], flags, after(shard.reshape(1), done), rows, stage.row, stage.row + stage.rows, b_k,
            b_cuts[: b_counts[h] + 1], b_dense[h],
        )
        return done

    def across(part, hop):
        return lax.ppermute(part, "row", [(r, (r + pair * hop) % rows) for r in range(rows)])

    hops = range(1, rows // pair)
    shards = [lax.rem(me_row - pair * hop + rows, rows) for hop in range(rows // pair)]
    came = {(0, hop): across(b_parts[0], hop) for hop in hops}
    lists = {0: b_parts}
    if pair == 2:
        lists[1] = [lax.ppermute(part, "row", swap) for part in b_parts]
    for side in range(pair):
        for h in range(len(b_stages)):
            done = unpack(h, shards[0] ^ side, lists[side], done)
    sides = {}
    for hop in hops:
        here = after(came[0, hop], done)
        sides[hop] = [[here], [lax.ppermute(here, "row", swap)]][:pair]
        for i in range(1, len(b_parts)):
            came[i, hop] = across(after(b_parts[i], here), hop)
    for side in range(pair):
        for hop in hops:
            done = unpack(0, shards[hop] ^ side, sides[hop][side], done)

    a_columns = jnp.arange(cols, dtype=jnp.int32)
    a_flags = gathered[:, 0, :a_rows, :a_k].astype(jnp.int32).reshape(cols * a_rows, a_k)

    a_marks = gathered[:, 0, :, 0].astype(jnp.int32)

    over = jnp.max(gathered[:, 0, mark_row(0) : mark_row(0) + 8].astype(jnp.float32), axis=0)

    def product_of(g, halves, done, **more):
        return multiply(
            joint, a_flags, a_marks, after(turn, done), a_columns, a_place, a_stages[: g + 1], a_k, a_cuts[: g + 2],
            halves, **more
        )

    high = piece * BLOCK + 16
    received = [[] for _ in range(layers - 1)]
    for h in range(len(b_stages)):
        if h:
            for hop in hops:
                here = [after(came[i, hop], done) for i in range(1, b_counts[h])]
                there = [lax.ppermute(part, "row", swap) for part in here]
                for side, more in zip(range(pair), (here, there)):
                    done = unpack(h, shards[hop] ^ side, sides[hop][side] + more, done)
            over = largest_over(after(over, codes[-16:, :BLOCK]), "row", rows, 2)
        codes = product_of(0, [b_dense[h]], done, over=over, pieces=layers - 1)
        if not h:
            over = largest_over(over, "row", rows, 1, 2)
        done = codes[-16:, :BLOCK]
        for q in range(layers - 1):
            there = [(i, (i + 1 + q) % layers) for i in range(layers)]
            received[q].append(lax.ppermute(codes[q * high : (q + 1) * high], "layer", there))

    product = product_of(1, b_dense, done, over=over)
    for g in range(2, len(a_stages)):
        last = g == len(a_stages) - 1
        product = product_of(g, b_dense, done, over=over, received=received if last else (), before=(product,))
    over = over[0, 0]
    for pairs in received:
        over = jnp.maximum(over, pairs[-1][-1, 0].astype(jnp.float32))
    return lax.cond(
        over > 0,
        lambda: whole_slab(a_tiles, a_occupancy, b_tiles, b_occupancy),
        lambda: product,
    )


def solution(mesh):
    sizes = tuple(mesh.shape[axis] for axis in ("row", "col", "layer"))
    in_specs = (
        P("row", ("layer", "col")),
        P("row", ("layer", "col")),
        P(("layer", "row"), "col"),
        P(("layer", "row"), "col"),
    )
    out_specs = P(("row", "layer"), "col")
    return jax.shard_map(
        functools.partial(per_device, sizes), mesh=mesh, in_specs=in_specs, out_specs=out_specs, check_vma=False
    )
```

```python
import functools
import math
import typing

import jax
import jax.numpy as jnp
from jax import lax
from jax.experimental import pallas as pl
from jax.experimental.pallas import tpu as pltpu
from jax.sharding import PartitionSpec as P

BLOCK = 128
VMEM_LIMIT = 56 * 1024 * 1024
TILE_ROOM = 256 * 16
SMALL = pl.CostEstimate(flops=1, bytes_accessed=1, transcendentals=0)
LARGE = pl.CostEstimate(flops=10**12, bytes_accessed=1, transcendentals=0)


def keep_blocks(values, occupancy):
    height, breadth = values.shape
    tiled = values.reshape(height // BLOCK, BLOCK, breadth // BLOCK, BLOCK)
    flags = occupancy.astype(values.dtype)
    return (tiled * flags[:, None, :, None]).reshape(height, breadth)


def along(part, axis, size, dim):
    me, length = lax.axis_index(axis), part.shape[dim]
    shape = list(part.shape)
    shape[dim] *= size
    whole = lax.dynamic_update_slice_in_dim(jnp.zeros(shape, part.dtype), part, me * length, dim)
    for hop in range(1, size):
        came = lax.ppermute(part, axis, [(i, (i + hop) % size) for i in range(size)])
        whole = lax.dynamic_update_slice_in_dim(whole, came, (me - hop + size) % size * length, dim)
    return whole


def whole_slab(sizes, a_tiles, a_occupancy, b_tiles, b_occupancy):
    rows, cols, layers = sizes
    a_slab = along(keep_blocks(a_tiles, a_occupancy), "col", cols, 1)
    b_kept = keep_blocks(b_tiles, b_occupancy)
    partial_value = jnp.zeros((a_slab.shape[0], b_kept.shape[1]), jnp.float32)
    for hop in range(rows):
        part = lax.ppermute(b_kept, "row", [(i, (i + hop) % rows) for i in range(rows)]) if hop else b_kept
        at = (lax.axis_index("row") - hop + rows) % rows * part.shape[0]
        beside = lax.dynamic_slice_in_dim(a_slab, at, part.shape[0], 1)
        partial_value += jnp.dot(beside, part, preferred_element_type=jnp.float32)
    me, length = lax.axis_index("layer"), partial_value.shape[0] // layers
    total = lax.dynamic_slice_in_dim(partial_value, me * length, length)
    for hop in range(1, layers):
        given = lax.dynamic_slice_in_dim(partial_value, (me + hop) % layers * length, length)
        total += lax.ppermute(given, "layer", [(i, (i + hop) % layers) for i in range(layers)])
    return total


def slots_for(blocks, spread):
    if blocks < 16:
        return blocks + 1
    room = (blocks * 7 + 15) // 16 + int(round(spread * blocks**0.5))
    return min(blocks, room) + 1


def cuts_for(stages, spread):
    cuts, blocks = [0], 0
    for stage in stages:
        blocks += stage.rows * stage.wide
        cuts.append(max(slots_for(blocks, spread), cuts[-1] + 1))
    return cuts


class Stage(typing.NamedTuple):
    row: int
    rows: int
    first: int
    wide: int


def header_of(occupancy):
    rows, columns = occupancy.shape
    flags = occupancy.astype(jnp.bfloat16)
    return jnp.pad(flags, ((0, BLOCK - rows), (0, BLOCK - columns)))


MARKS, OVER = BLOCK - 8, BLOCK - 1


def pack_kernel(place, stages, ends, cuts, other, columns, turn_ref, flags_ref, other_ref, header_ref, values_ref, *refs):
    n = len(cuts) - 1
    parts, (whole, held, sem, out_sems) = refs[:n], refs[-4:]
    header = pltpu.make_async_copy(header_ref.at[:BLOCK, :BLOCK], held.at[0], sem)
    if other is None:
        header.start()
    else:
        held[0] = jnp.zeros_like(held[0])
    lane = lax.broadcasted_iota(jnp.int32, (16, BLOCK), 1)

    def step_of(stage):
        def step(u, carry):
            slot, notes = carry
            row, column = place(stage, u, turn_ref[0])
            flag = flags_ref[row, column]

            @pl.when(flag > 0)
            def _():
                pltpu.make_async_copy(
                    values_ref.at[
                        pl.ds(pl.multiple_of(row * BLOCK, BLOCK), BLOCK),
                        pl.ds(pl.multiple_of(column * BLOCK, BLOCK), BLOCK),
                    ],
                    held.at[jnp.minimum(slot, cuts[-1])],
                    sem,
                ).start()

            if other is not None:
                code = (stage.row + u // stage.wide) * columns + stage.first + u % stage.wide
                notes = jnp.where(lane == jnp.where(flag > 0, slot, BLOCK), code.astype(jnp.float32), notes)
            return slot + flag, notes

        return step

    slot, over, marks = jnp.int32(1), jnp.int32(0), []
    notes = jnp.zeros((16, BLOCK), jnp.float32)
    for stage, cut in zip(stages, ends[1:]):
        marks.append(slot)
        slot, notes = lax.fori_loop(0, stage.rows * stage.wide, step_of(stage), (slot, notes), unroll=4)
        over = jnp.maximum(over, jnp.where(slot > cut, 1, 0))
    marks.append(slot)
    if other is not None:
        other_place, other_stages, other_ends = other
        spent = jnp.int32(1)
        for stage, cut in zip(other_stages, other_ends[1:]):

            def count(u, spent):
                row, column = other_place(stage, u, turn_ref[0])
                return spent + other_ref[row, column]

            spent = lax.fori_loop(0, stage.rows * stage.wide, count, spent, unroll=16)
            over = jnp.maximum(over, jnp.where(spent > cut, 1, 0))

    def settle(t, _):
        header.wait()
        return 0

    lax.fori_loop(0, slot if other is None else slot - 1, settle, 0)
    if other is not None:
        notes = jnp.where(lane >= MARKS, over.astype(jnp.float32), notes)
        for i, mark in enumerate(marks):
            notes = jnp.where(lane == MARKS + i, mark.astype(jnp.float32), notes)
        held[0, :16, :] = notes.astype(held.dtype)
    copies = [
        pltpu.make_async_copy(held.at[pl.ds(lo, hi - lo)], part, out_sems.at[i])
        for i, (part, lo, hi) in enumerate(zip(parts, cuts[:-1], cuts[1:]))
    ]
    if other is None:
        copies.append(pltpu.make_async_copy(held.at[pl.ds(0, cuts[-1])], whole, out_sems.at[n]))
    for copy in copies:
        copy.start()
    for copy in copies:
        copy.wait()


def pack(values, occupancy, turn, place, stages, ends, cuts, other_flags, other):
    n = len(cuts) - 1
    sizes = [hi - lo for lo, hi in zip(cuts[:-1], cuts[1:])] + [cuts[-1] if other is None else 1]
    if other is None:
        header = header_of(occupancy)
    else:
        header = values
        assert cuts[-1] <= MARKS and len(stages) < OVER - MARKS and occupancy.size <= 256
    *parts, whole = pl.pallas_call(
        functools.partial(pack_kernel, place, stages, ends, cuts, other, occupancy.shape[1]),
        grid_spec=pltpu.PrefetchScalarGridSpec(
            num_scalar_prefetch=3,
            grid=(),
            in_specs=[pl.BlockSpec(memory_space=pl.ANY)] * 2,
            out_specs=[pl.BlockSpec(memory_space=pl.ANY)] * (n + 1),
            scratch_shapes=[
                pltpu.VMEM((cuts[-1] + 1, BLOCK, BLOCK), values.dtype),
                pltpu.SemaphoreType.DMA,
                pltpu.SemaphoreType.DMA((n + 1,)),
            ],
        ),
        out_shape=[jax.ShapeDtypeStruct((size, BLOCK, BLOCK), values.dtype) for size in sizes],
        compiler_params=pltpu.CompilerParams(vmem_limit_bytes=VMEM_LIMIT),
        cost_estimate=SMALL,
        name="pack",
    )(turn, occupancy, other_flags, header, values)
    return parts, whole


def after(values, others):
    k = len(values)
    whole = pl.BlockSpec(memory_space=pl.ANY)
    return pl.pallas_call(
        lambda *refs: None,
        in_specs=[whole] * (k + len(others)),
        out_specs=[whole] * k,
        out_shape=[jax.ShapeDtypeStruct(value.shape, value.dtype) for value in values],
        input_output_aliases={i: i for i in range(k)},
        cost_estimate=SMALL,
        name="after",
    )(*values, *others)


def load_list(parts, cuts, held, sems):
    return [
        pltpu.make_async_copy(part, held.at[pl.ds(lo, hi - lo)], sems.at[i])
        for i, (part, lo, hi) in enumerate(zip(parts, cuts[:-1], cuts[1:]))
    ]


def unpack_b_kernel(k_blocks, first, stop, cuts, shard_ref, flags_ref, *refs):
    parts, (out_ref, done_ref, held, sems, sem) = refs[: len(cuts) - 1], refs[-5:]
    done_ref[0] = 0
    nothing = cuts[-1]
    copies = load_list(parts, cuts, held, sems)
    for copy in copies:
        copy.start()
    held[nothing] = jnp.zeros_like(held[nothing])

    def flag_of(t):
        return flags_ref[t % k_blocks, t // k_blocks]

    slot = lax.fori_loop(0, first * k_blocks, lambda t, slot: slot + flag_of(t), jnp.int32(1), unroll=8)
    for copy in copies:
        copy.wait()
    base = shard_ref[0] * k_blocks

    def step(t, slot):
        flag = flag_of(first * k_blocks + t)
        pltpu.make_async_copy(
            held.at[jnp.where(flag > 0, jnp.minimum(slot, nothing), nothing)],
            out_ref.at[
                pl.ds(pl.multiple_of((base + t % k_blocks) * BLOCK, BLOCK), BLOCK),
                pl.ds(pl.multiple_of(t // k_blocks * BLOCK, BLOCK), BLOCK),
            ],
            sem,
        ).start()
        return slot + flag

    lax.fori_loop(0, (stop - first) * k_blocks, step, slot, unroll=8)
    written = out_ref.at[pl.ds(pl.multiple_of(base * BLOCK, BLOCK), k_blocks * BLOCK)]
    pltpu.make_async_copy(written, written, sem).wait()


def unpack_b(parts, flags, shard, shards, first, stop, k_blocks, cuts, into, token):
    n = len(parts)
    operands = [*parts, token] + ([] if into is None else [into])
    return pl.pallas_call(
        functools.partial(unpack_b_kernel, k_blocks, first, stop, cuts),
        grid_spec=pltpu.PrefetchScalarGridSpec(
            num_scalar_prefetch=2,
            grid=(),
            in_specs=[pl.BlockSpec(memory_space=pl.ANY)] * len(operands),
            out_specs=[pl.BlockSpec(memory_space=pl.ANY), pl.BlockSpec(memory_space=pltpu.SMEM)],
            scratch_shapes=[
                pltpu.VMEM((cuts[-1] + 1, BLOCK, BLOCK), parts[0].dtype),
                pltpu.SemaphoreType.DMA((n,)),
                pltpu.SemaphoreType.DMA,
            ],
        ),
        out_shape=[
            jax.ShapeDtypeStruct((shards * k_blocks * BLOCK, (stop - first) * BLOCK), parts[0].dtype),
            jax.ShapeDtypeStruct((1,), jnp.int32),
        ],
        input_output_aliases={} if into is None else {3 + n: 0},
        compiler_params=pltpu.CompilerParams(vmem_limit_bytes=VMEM_LIMIT),
        cost_estimate=SMALL,
        name="unpack_b",
    )(shard, flags, *operands)


def multiply_kernel(plan, notes_ref, *refs):
    stages, k_blocks, cuts, shards, halves, given, carried, tokens, pieces, starts, ends = plan
    stage, g = stages[-1], len(stages) - 1
    rows, wide = stage.rows, stage.wide
    n = len(cuts) - 1
    parts, refs = refs[:n], refs[n:]
    b_refs, refs = refs[:halves], refs[halves:]
    codes_in, refs = refs[: halves * given], refs[halves * given :]
    before, refs = refs[:carried], refs[carried + tokens :]
    over_ref, out_ref, dense, sem, total = refs

    def fill():
        dense[...] = jnp.zeros_like(dense)
        started = jnp.int32(0)
        for s in range(shards):
            base = s * wide - stage.first

            for part, lo, hi in zip(parts, cuts[:-1], cuts[1:]):

                def put(slot, _):
                    code = notes_ref[s, slot]
                    row, k = lax.div(code, k_blocks), lax.rem(code, k_blocks)
                    pltpu.make_async_copy(
                        part.at[s, slot - lo],
                        dense.at[
                            pl.ds(pl.multiple_of((row - stage.row) * BLOCK, BLOCK), BLOCK),
                            pl.ds(pl.multiple_of((base + k) * BLOCK, BLOCK), BLOCK),
                        ],
                        sem,
                    ).start()
                    return 0

                first = jnp.maximum(notes_ref[s, MARKS + g], lo)
                stop = jnp.maximum(jnp.minimum(notes_ref[s, MARKS + g + 1], hi), first)
                lax.fori_loop(first, stop, put, 0)
                started += stop - first

        def settle(t, _):
            pltpu.make_async_copy(parts[0].at[0, 0], dense.at[:BLOCK, :BLOCK], sem).wait()
            return 0

        lax.fori_loop(0, started, settle, 0)

    pl.when(pl.program_id(0) == 0)(fill)

    def code(value):
        share = rows // pieces
        for q in range(pieces):
            base = q * (share * BLOCK + 16)
            powers = []
            for r in range(share):
                some = value[(q * share + r) * BLOCK : (q * share + r + 1) * BLOCK]
                top = jnp.max(jnp.abs(some), axis=0, keepdims=True)
                power = jnp.clip(jnp.ceil(jnp.log2(top)), -60.0, 60.0)
                some = jnp.clip(jnp.round(some * jnp.exp2(15.0 - power)), -32767.0, 32767.0)
                out_ref[base + r * BLOCK : base + (r + 1) * BLOCK] = some.astype(jnp.int32).astype(jnp.int16)
                powers.append(power)
            flag = jnp.broadcast_to(over_ref[0:1, 0:1], powers[0].shape)
            notes = jnp.concatenate(powers + [flag] * (16 - share), axis=0)
            out_ref[base + share * BLOCK : base + share * BLOCK + 16] = notes.astype(jnp.int32).astype(jnp.int16)

    def finish(value, h):
        for r in range(rows):
            span = slice(r * BLOCK, (r + 1) * BLOCK)
            some = value[span]
            for q in range(given):
                codes = codes_in[q * halves + h]
                notes = codes[rows * BLOCK : rows * BLOCK + 16].astype(jnp.int32).astype(jnp.float32)
                some += codes[span].astype(jnp.int32).astype(jnp.float32) * jnp.exp2(notes[r : r + 1] - 15.0)
            for earlier in before:
                some += earlier[span]
            out_ref[span] = some

    for h, b_ref in enumerate(b_refs):

        @pl.when((pl.program_id(0) >= starts[h]) & (pl.program_id(0) < ends[h]))
        def _():
            b_here = b_ref[...].reshape(-1, b_ref.shape[-1])
            total[...] = jnp.dot(dense[...], b_here, preferred_element_type=jnp.float32)
            if pieces:
                code(total)
            else:
                finish(total, h)


def multiply(
    parts, notes, stages, k_blocks, cuts, b_halves, over, pieces=0, received=(), before=(), tokens=()
):
    shards, halves = parts[0].shape[0], len(b_halves)
    stage = stages[-1]
    n = len(cuts) - 1
    widths = [b_half.shape[1] for b_half in b_halves]
    shared = math.gcd(*widths)
    tile = max(t for t in (BLOCK, 256, 512) if shared % t == 0 and t * stage.wide <= TILE_ROOM)
    ends = [sum(widths[: h + 1]) // tile for h in range(halves)]
    starts = [0] + ends[:-1]
    deep = math.gcd(math.gcd(stage.first, stage.wide), k_blocks)
    layers, skip = stage.wide // deep, stage.first // deep
    assert skip % layers == 0
    tall = stage.rows * BLOCK
    whole = pl.BlockSpec(memory_space=pl.ANY)

    def at(h, *fixed):
        return lambda j, *_: (*fixed, jnp.clip(j - starts[h], 0, ends[h] - starts[h] - 1))

    in_specs = [whole] * n
    operands = [*parts[:n]]
    for h, b_half in enumerate(b_halves):
        in_specs.append(pl.BlockSpec((shards, layers, deep * BLOCK, tile), at(h, 0, skip // layers, 0)))
        operands.append(b_half.reshape(shards, k_blocks // deep, deep * BLOCK, widths[h]))
    for pairs in received:
        for h, codes in enumerate(pairs):
            in_specs.append(pl.BlockSpec((tall + 16, tile), at(h, 0)))
            operands.append(codes)
    in_specs += [pl.BlockSpec((tall, tile), lambda j, *_: (0, j))] * len(before)
    operands += [*before]
    in_specs += [whole] * len(tokens) + [pl.BlockSpec(memory_space=pltpu.VMEM)]
    operands += [*tokens, over]
    high = tall + 16 * pieces
    plan = (stages, k_blocks, cuts, shards, halves, len(received), len(before), len(tokens), pieces, starts, ends)
    return pl.pallas_call(
        functools.partial(multiply_kernel, plan),
        grid_spec=pltpu.PrefetchScalarGridSpec(
            num_scalar_prefetch=1,
            grid=(ends[-1],),
            in_specs=in_specs,
            out_specs=pl.BlockSpec((high, tile), lambda j, *_: (0, j)),
            scratch_shapes=[
                pltpu.VMEM((tall, shards * stage.wide * BLOCK), b_halves[0].dtype),
                pltpu.SemaphoreType.DMA,
                pltpu.VMEM((tall, tile), jnp.float32),
            ],
        ),
        out_shape=jax.ShapeDtypeStruct((high, sum(widths)), jnp.int16 if pieces else jnp.float32),
        compiler_params=pltpu.CompilerParams(vmem_limit_bytes=VMEM_LIMIT),
        cost_estimate=SMALL,
        name="multiply",
    )(notes, *operands)


def largest_over(value, axis, size):
    step = 1
    while step < size:
        value = jnp.maximum(value, lax.ppermute(value, axis, [(i, i ^ step) for i in range(size)]))
        step *= 2
    return value


def per_device(sizes, a_tiles, a_occupancy, b_tiles, b_occupancy):
    rows, cols, layers = sizes
    me_row, me_col, me_layer = (lax.axis_index(axis).astype(jnp.int32) for axis in ("row", "col", "layer"))
    a_rows, a_k = a_occupancy.shape
    b_k, b_columns = b_occupancy.shape
    piece = a_rows // layers
    given = a_rows - piece
    turn = me_layer.reshape(1)

    def a_place(stage, u, layer):
        row, k = stage.row + u // stage.wide, stage.first + u % stage.wide
        return lax.rem(row + (layer + 1) * piece, a_rows), k

    def b_place(stage, u, _):
        return stage.first + u % stage.wide, stage.row + u // stage.wide

    early = a_k * 3 // 4
    a_stages = [Stage(0, given, 0, a_k), Stage(given, piece, 0, early), Stage(given, piece, early, a_k - early)]
    half = b_columns * 5 // 8
    b_stages = [Stage(0, half, 0, b_k), Stage(half, b_columns - half, 0, b_k)]
    a_cuts, b_cuts = cuts_for(a_stages, 1.77), cuts_for(b_stages, 2.0)

    a_parts, _ = pack(a_tiles, a_occupancy, turn, a_place, a_stages, a_cuts, a_cuts, b_occupancy, (b_place, b_stages, b_cuts))
    a_parts = [lax.all_gather(part, "col", axis=0) for part in a_parts]
    b_parts, b_whole = pack(b_tiles, b_occupancy, turn, b_place, b_stages, b_cuts, b_cuts, b_occupancy, None)

    pair = 2 if rows % 2 == 0 else 1
    swap = [(r, r ^ 1) for r in range(rows)]
    hops = range(1, rows // pair)
    shards = [lax.rem(me_row - pair * hop + rows, rows) for hop in range(rows // pair)]
    b_dense = [None] * len(b_stages)

    def across(part, hop):
        return lax.ppermute(part, "row", [(r, (r + pair * hop) % rows) for r in range(rows)])

    def unpack(h, shard, parts, cuts, token):
        stage = b_stages[h]
        flags = parts[0][0, :b_k, :b_columns].astype(jnp.int32)
        b_dense[h], token = unpack_b(
            parts, flags, shard.reshape(1), rows, stage.row, stage.row + stage.rows, b_k, cuts, b_dense[h], token
        )
        return token

    came = [across(b_parts[0], hop) for hop in hops]
    cut = [0, b_cuts[-1]]
    token = turn
    for h in range(2):
        token = unpack(h, shards[0], [b_whole], cut, token)
    if pair == 2:
        other = lax.ppermute(b_whole, "row", swap)
        for h in range(2):
            token = unpack(h, shards[0] ^ 1, [other], cut, token)

    *came, b_second = after([*came, b_parts[1]], [token])
    sides = [[part] for part in came]
    if pair == 2:
        sides += [[lax.ppermute(part, "row", swap)] for part in came]
    came = [across(b_second, hop) for hop in hops]
    places = [shards[hop] ^ side for side in range(pair) for hop in hops]
    for place, parts in zip(places, sides):
        token = unpack(0, place, parts, b_cuts[:2], token)
    notes = a_parts[0][:, 0, 0].astype(jnp.int32)
    over = jnp.max(a_parts[0][:, 0, :8, MARKS:].astype(jnp.float32), axis=0)[:, OVER - MARKS :]
    over = jnp.broadcast_to(over, (8, BLOCK))

    def product_of(g, halves, over, **more):
        return multiply(a_parts, notes, a_stages[: g + 1], a_k, a_cuts[: g + 2], halves, over, **more)

    high = piece * BLOCK + 16

    def exchange(codes):
        out = []
        for q in range(layers - 1):
            there = [(i, (i + 1 + q) % layers) for i in range(layers)]
            out.append(lax.ppermute(codes[q * high : (q + 1) * high], "layer", there))
        return out

    codes = product_of(0, b_dense[:1], over, pieces=layers - 1, tokens=[token])

    came = after(came, [codes])
    first = exchange(codes)
    more = [*came]
    if pair == 2:
        more += [lax.ppermute(part, "row", swap) for part in came]
    for place, parts, part in zip(places, sides, more):
        token = unpack(1, place, [*parts, part], b_cuts, token)
    over = largest_over(over, "row", rows)
    codes = product_of(0, b_dense[1:], over, pieces=layers - 1, tokens=[token])

    second = exchange(codes)
    product = product_of(1, b_dense, over, tokens=[codes])

    received = [*zip(first, second)]
    product = product_of(2, b_dense, over, received=received, before=(product,))
    over = over[0, 0]
    for codes in second:
        over = jnp.maximum(over, codes[-1, 0].astype(jnp.float32))
    return lax.cond(
        over > 0,
        lambda: whole_slab(sizes, a_tiles, a_occupancy, b_tiles, b_occupancy),
        lambda: product,
    )


def solution(mesh):
    sizes = tuple(mesh.shape[axis] for axis in ("row", "col", "layer"))
    in_specs = (
        P("row", ("layer", "col")),
        P("row", ("layer", "col")),
        P(("layer", "row"), "col"),
        P(("layer", "row"), "col"),
    )
    out_specs = P(("row", "layer"), "col")
    return jax.shard_map(
        functools.partial(per_device, sizes), mesh=mesh, in_specs=in_specs, out_specs=out_specs, check_vma=False
    )
```

```python
import functools
import math
import typing

import jax
import jax.numpy as jnp
from jax import lax
from jax.experimental import pallas as pl
from jax.experimental.pallas import tpu as pltpu
from jax.sharding import PartitionSpec as P

BLOCK = 128
VMEM_LIMIT = 63 * 1024 * 1024
TILE_ROOM = 256 * 16
SMALL = pl.CostEstimate(flops=1, bytes_accessed=1, transcendentals=0)
LARGE = pl.CostEstimate(flops=10**12, bytes_accessed=1, transcendentals=0)


def keep_blocks(values, occupancy):
    height, breadth = values.shape
    tiled = values.reshape(height // BLOCK, BLOCK, breadth // BLOCK, BLOCK)
    flags = occupancy.astype(values.dtype)
    return (tiled * flags[:, None, :, None]).reshape(height, breadth)


def along(part, axis, size, dim):
    me, length = lax.axis_index(axis), part.shape[dim]
    shape = list(part.shape)
    shape[dim] *= size
    whole = lax.dynamic_update_slice_in_dim(jnp.zeros(shape, part.dtype), part, me * length, dim)
    for hop in range(1, size):
        came = lax.ppermute(part, axis, [(i, (i + hop) % size) for i in range(size)])
        whole = lax.dynamic_update_slice_in_dim(whole, came, (me - hop + size) % size * length, dim)
    return whole


def whole_slab(sizes, a_tiles, a_occupancy, b_tiles, b_occupancy):
    rows, cols, layers = sizes
    a_slab = along(keep_blocks(a_tiles, a_occupancy), "col", cols, 1)
    b_kept = keep_blocks(b_tiles, b_occupancy)
    partial_value = jnp.zeros((a_slab.shape[0], b_kept.shape[1]), jnp.float32)
    for hop in range(rows):
        part = lax.ppermute(b_kept, "row", [(i, (i + hop) % rows) for i in range(rows)]) if hop else b_kept
        at = (lax.axis_index("row") - hop + rows) % rows * part.shape[0]
        beside = lax.dynamic_slice_in_dim(a_slab, at, part.shape[0], 1)
        partial_value += jnp.dot(beside, part, preferred_element_type=jnp.float32)
        partial_value, b_kept = lax.optimization_barrier((partial_value, b_kept))
    me, length = lax.axis_index("layer"), partial_value.shape[0] // layers
    total = lax.dynamic_slice_in_dim(partial_value, me * length, length)
    for hop in range(1, layers):
        given = lax.dynamic_slice_in_dim(partial_value, (me + hop) % layers * length, length)
        total += lax.ppermute(given, "layer", [(i, (i + hop) % layers) for i in range(layers)])
    return total


def slots_for(blocks, spread):
    if blocks < 16:
        return blocks + 1
    room = (blocks * 7 + 15) // 16 + int(round(spread * blocks**0.5))
    return min(blocks, room) + 1


def cuts_for(stages, spread):
    cuts, blocks = [0], 0
    for stage in stages:
        blocks += stage.rows * stage.wide
        cuts.append(max(slots_for(blocks, spread), cuts[-1] + 1))
    return cuts


class Stage(typing.NamedTuple):
    row: int
    rows: int
    first: int
    wide: int


def header_of(occupancy):
    rows, columns = occupancy.shape
    flags = occupancy.astype(jnp.bfloat16)
    return jnp.pad(flags, ((0, BLOCK - rows), (0, BLOCK - columns)))


MARKS, OVER = BLOCK - 8, BLOCK - 1


def pack_kernel(place, stages, ends, cuts, other, columns, turn_ref, flags_ref, other_ref, header_ref, values_ref, *refs):
    n = len(cuts) - 1
    parts, (whole, held, sem, out_sems) = refs[:n], refs[-4:]
    header = pltpu.make_async_copy(header_ref.at[:BLOCK, :BLOCK], held.at[0], sem)
    if other is None:
        header.start()
    else:
        held[0] = jnp.zeros_like(held[0])
    lane = lax.broadcasted_iota(jnp.int32, (16, BLOCK), 1)

    def step_of(stage):
        def step(u, carry):
            slot, notes = carry
            row, column = place(stage, u, turn_ref[0])
            flag = flags_ref[row, column]

            @pl.when(flag > 0)
            def _():
                pltpu.make_async_copy(
                    values_ref.at[
                        pl.ds(pl.multiple_of(row * BLOCK, BLOCK), BLOCK),
                        pl.ds(pl.multiple_of(column * BLOCK, BLOCK), BLOCK),
                    ],
                    held.at[jnp.minimum(slot, cuts[-1])],
                    sem,
                ).start()

            if other is not None:
                code = (stage.row + u // stage.wide) * columns + stage.first + u % stage.wide
                notes = jnp.where(lane == jnp.where(flag > 0, slot, BLOCK), code.astype(jnp.float32), notes)
            return slot + flag, notes

        return step

    slot, over, marks = jnp.int32(1), jnp.int32(0), []
    notes = jnp.zeros((16, BLOCK), jnp.float32)
    for stage, cut in zip(stages, ends[1:]):
        marks.append(slot)
        slot, notes = lax.fori_loop(0, stage.rows * stage.wide, step_of(stage), (slot, notes), unroll=4)
        over = jnp.maximum(over, jnp.where(slot > cut, 1, 0))
    marks.append(slot)
    if other is not None:
        other_place, other_stages, other_ends = other
        spent = jnp.int32(1)
        for stage, cut in zip(other_stages, other_ends[1:]):

            def count(u, spent):
                row, column = other_place(stage, u, turn_ref[0])
                return spent + other_ref[row, column]

            spent = lax.fori_loop(0, stage.rows * stage.wide, count, spent, unroll=16)
            over = jnp.maximum(over, jnp.where(spent > cut, 1, 0))

    def settle(t, _):
        header.wait()
        return 0

    lax.fori_loop(0, slot if other is None else slot - 1, settle, 0)
    if other is not None:
        notes = jnp.where(lane >= MARKS, over.astype(jnp.float32), notes)
        for i, mark in enumerate(marks):
            notes = jnp.where(lane == MARKS + i, mark.astype(jnp.float32), notes)
        held[0, :16, :] = notes.astype(held.dtype)
    copies = [
        pltpu.make_async_copy(held.at[pl.ds(lo, hi - lo)], part, out_sems.at[i])
        for i, (part, lo, hi) in enumerate(zip(parts, cuts[:-1], cuts[1:]))
    ]
    if other is None:
        copies.append(pltpu.make_async_copy(held.at[pl.ds(0, cuts[-1])], whole, out_sems.at[n]))
    for copy in copies:
        copy.start()
    for copy in copies:
        copy.wait()


def pack(values, occupancy, turn, place, stages, ends, cuts, other_flags, other):
    n = len(cuts) - 1
    sizes = [hi - lo for lo, hi in zip(cuts[:-1], cuts[1:])] + [cuts[-1] if other is None else 1]
    if other is None:
        header = header_of(occupancy)
    else:
        header = values
        assert cuts[-1] <= MARKS and len(stages) < OVER - MARKS and occupancy.size <= 256
    *parts, whole = pl.pallas_call(
        functools.partial(pack_kernel, place, stages, ends, cuts, other, occupancy.shape[1]),
        grid_spec=pltpu.PrefetchScalarGridSpec(
            num_scalar_prefetch=3,
            grid=(),
            in_specs=[pl.BlockSpec(memory_space=pl.ANY)] * 2,
            out_specs=[pl.BlockSpec(memory_space=pl.ANY)] * (n + 1),
            scratch_shapes=[
                pltpu.VMEM((cuts[-1] + 1, BLOCK, BLOCK), values.dtype),
                pltpu.SemaphoreType.DMA,
                pltpu.SemaphoreType.DMA((n + 1,)),
            ],
        ),
        out_shape=[jax.ShapeDtypeStruct((size, BLOCK, BLOCK), values.dtype) for size in sizes],
        compiler_params=pltpu.CompilerParams(vmem_limit_bytes=VMEM_LIMIT),
        cost_estimate=SMALL,
        name="pack",
    )(turn, occupancy, other_flags, header, values)
    return parts, whole


def after(values, others):
    k = len(values)
    whole = pl.BlockSpec(memory_space=pl.ANY)
    return pl.pallas_call(
        lambda *refs: None,
        in_specs=[whole] * (k + len(others)),
        out_specs=[whole] * k,
        out_shape=[jax.ShapeDtypeStruct(value.shape, value.dtype) for value in values],
        input_output_aliases={i: i for i in range(k)},
        cost_estimate=SMALL,
        name="after",
    )(*values, *others)


def load_list(parts, cuts, held, sems):
    return [
        pltpu.make_async_copy(part, held.at[pl.ds(lo, hi - lo)], sems.at[i])
        for i, (part, lo, hi) in enumerate(zip(parts, cuts[:-1], cuts[1:]))
    ]


def unpack_b_kernel(k_blocks, first, stop, cuts, shard_ref, flags_ref, *refs):
    parts, (out_ref, done_ref, held, sems, sem) = refs[: len(cuts) - 1], refs[-5:]
    done_ref[0] = 0
    nothing = cuts[-1]
    copies = load_list(parts, cuts, held, sems)
    for copy in copies:
        copy.start()
    held[nothing] = jnp.zeros_like(held[nothing])

    def flag_of(t):
        return flags_ref[t % k_blocks, t // k_blocks]

    slot = lax.fori_loop(0, first * k_blocks, lambda t, slot: slot + flag_of(t), jnp.int32(1), unroll=8)
    for copy in copies:
        copy.wait()
    base = shard_ref[0] * k_blocks

    def step(t, slot):
        flag = flag_of(first * k_blocks + t)
        pltpu.make_async_copy(
            held.at[jnp.where(flag > 0, jnp.minimum(slot, nothing), nothing)],
            out_ref.at[
                pl.ds(pl.multiple_of((base + t % k_blocks) * BLOCK, BLOCK), BLOCK),
                pl.ds(pl.multiple_of(t // k_blocks * BLOCK, BLOCK), BLOCK),
            ],
            sem,
        ).start()
        return slot + flag

    lax.fori_loop(0, (stop - first) * k_blocks, step, slot, unroll=8)
    written = out_ref.at[pl.ds(pl.multiple_of(base * BLOCK, BLOCK), k_blocks * BLOCK)]
    pltpu.make_async_copy(written, written, sem).wait()


def unpack_b(parts, flags, shard, shards, first, stop, k_blocks, cuts, into, tokens):
    n = len(parts)
    operands = [*parts, *tokens] + ([] if into is None else [into])
    return pl.pallas_call(
        functools.partial(unpack_b_kernel, k_blocks, first, stop, cuts),
        grid_spec=pltpu.PrefetchScalarGridSpec(
            num_scalar_prefetch=2,
            grid=(),
            in_specs=[pl.BlockSpec(memory_space=pl.ANY)] * len(operands),
            out_specs=[pl.BlockSpec(memory_space=pl.ANY), pl.BlockSpec(memory_space=pltpu.SMEM)],
            scratch_shapes=[
                pltpu.VMEM((cuts[-1] + 1, BLOCK, BLOCK), parts[0].dtype),
                pltpu.SemaphoreType.DMA((n,)),
                pltpu.SemaphoreType.DMA,
            ],
        ),
        out_shape=[
            jax.ShapeDtypeStruct((shards * k_blocks * BLOCK, (stop - first) * BLOCK), parts[0].dtype),
            jax.ShapeDtypeStruct((1,), jnp.int32),
        ],
        input_output_aliases={} if into is None else {2 + n + len(tokens): 0},
        compiler_params=pltpu.CompilerParams(vmem_limit_bytes=VMEM_LIMIT),
        cost_estimate=SMALL,
        name="unpack_b",
    )(shard, flags, *operands)


def multiply_kernel(plan, notes_ref, hop_ref, *refs):
    stages, k_blocks, cuts, shards, halves, given, carried, tokens, pieces, remarks, starts, ends = plan
    stage, g = stages[-1], len(stages) - 1
    rows, wide = stage.rows, stage.wide
    n = len(cuts) - 1
    parts, refs = refs[:n], refs[n:]
    b_refs, refs = refs[:halves], refs[halves:]
    codes_in, refs = refs[: halves * given], refs[halves * given :]
    before, refs = refs[:carried], refs[carried + tokens :]
    over_ref, out_ref, dense, sem, total = refs

    def fill():
        dense[...] = jnp.zeros_like(dense)
        started = jnp.int32(0)
        for s in range(shards):
            base, hop = s * wide - stage.first, hop_ref[s]

            for part, at, lo, hi in zip(parts, [hop] + [s] * (n - 1), cuts[:-1], cuts[1:]):

                def put(slot, _):
                    code = notes_ref[hop, slot]
                    row, k = lax.div(code, k_blocks), lax.rem(code, k_blocks)
                    pltpu.make_async_copy(
                        part.at[at, slot - lo],
                        dense.at[
                            pl.ds(pl.multiple_of((row - stage.row) * BLOCK, BLOCK), BLOCK),
                            pl.ds(pl.multiple_of((base + k) * BLOCK, BLOCK), BLOCK),
                        ],
                        sem,
                    ).start()
                    return 0

                first = jnp.maximum(notes_ref[hop, MARKS + g], lo)
                stop = jnp.maximum(jnp.minimum(notes_ref[hop, MARKS + g + 1], hi), first)
                lax.fori_loop(first, stop, put, 0)
                started += stop - first

        def settle(t, _):
            pltpu.make_async_copy(parts[0].at[0, 0], dense.at[:BLOCK, :BLOCK], sem).wait()
            return 0

        lax.fori_loop(0, started, settle, 0)

    pl.when(pl.program_id(0) == 0)(fill)

    def code(value):
        share = rows // pieces
        for q in range(pieces):
            base = q * (share * BLOCK + remarks)
            powers = []
            for r in range(share):
                some = value[(q * share + r) * BLOCK : (q * share + r + 1) * BLOCK]
                top = jnp.max(jnp.abs(some), axis=0, keepdims=True)
                power = jnp.clip(jnp.ceil(jnp.log2(top)), -60.0, 60.0)
                some = jnp.clip(jnp.round(some * jnp.exp2(15.0 - power)), -32767.0, 32767.0)
                out_ref[base + r * BLOCK : base + (r + 1) * BLOCK] = some.astype(jnp.int32).astype(jnp.int16)
                powers.append(power)
            flag = jnp.broadcast_to(over_ref[0:1, 0:1], powers[0].shape)
            notes = jnp.concatenate(powers + [flag] * (remarks - share), axis=0)
            out_ref[base + share * BLOCK : base + share * BLOCK + remarks] = notes.astype(jnp.int32).astype(jnp.int16)

    def finish(value, h):
        for r in range(rows):
            span = slice(r * BLOCK, (r + 1) * BLOCK)
            some = value[span]
            for q in range(given):
                codes = codes_in[q * halves + h]
                notes = codes[rows * BLOCK : rows * BLOCK + 16].astype(jnp.int32).astype(jnp.float32)
                some += codes[span].astype(jnp.int32).astype(jnp.float32) * jnp.exp2(notes[r : r + 1] - 15.0)
            for earlier in before:
                some += earlier[span]
            out_ref[span] = some

    for h, b_ref in enumerate(b_refs):

        @pl.when((pl.program_id(0) >= starts[h]) & (pl.program_id(0) < ends[h]))
        def _():
            b_here = b_ref[...].reshape(-1, b_ref.shape[-1])
            total[...] = jnp.dot(dense[...], b_here, preferred_element_type=jnp.float32)
            if pieces:
                code(total)
            else:
                finish(total, h)


def multiply(
    parts, notes, hops, stages, k_blocks, cuts, b_halves, over, pieces=0, remarks=16, received=(), before=(), tokens=()
):
    shards, halves = parts[0].shape[0], len(b_halves)
    stage = stages[-1]
    n = len(cuts) - 1
    widths = [b_half.shape[1] for b_half in b_halves]
    shared = math.gcd(*widths)
    tile = max(t for t in (BLOCK, 256, 512) if shared % t == 0 and t * stage.wide <= TILE_ROOM)
    ends = [sum(widths[: h + 1]) // tile for h in range(halves)]
    starts = [0] + ends[:-1]
    deep = math.gcd(math.gcd(stage.first, stage.wide), k_blocks)
    layers, skip = stage.wide // deep, stage.first // deep
    assert skip % layers == 0
    tall = stage.rows * BLOCK
    whole = pl.BlockSpec(memory_space=pl.ANY)

    def at(h, *fixed):
        return lambda j, *_: (*fixed, jnp.clip(j - starts[h], 0, ends[h] - starts[h] - 1))

    in_specs = [whole] * n
    operands = [*parts[:n]]
    for h, b_half in enumerate(b_halves):
        in_specs.append(pl.BlockSpec((shards, layers, deep * BLOCK, tile), at(h, 0, skip // layers, 0)))
        operands.append(b_half.reshape(shards, k_blocks // deep, deep * BLOCK, widths[h]))
    for pairs in received:
        for h, codes in enumerate(pairs):
            in_specs.append(pl.BlockSpec((codes.shape[0], tile), at(h, 0)))
            operands.append(codes)
    in_specs += [pl.BlockSpec((tall, tile), lambda j, *_: (0, j))] * len(before)
    operands += [*before]
    in_specs += [whole] * len(tokens) + [pl.BlockSpec(memory_space=pltpu.VMEM)]
    operands += [*tokens, over]
    high = tall + remarks * pieces
    plan = (stages, k_blocks, cuts, shards, halves, len(received), len(before), len(tokens), pieces, remarks, starts, ends)
    return pl.pallas_call(
        functools.partial(multiply_kernel, plan),
        grid_spec=pltpu.PrefetchScalarGridSpec(
            num_scalar_prefetch=2,
            grid=(ends[-1],),
            in_specs=in_specs,
            out_specs=pl.BlockSpec((high, tile), lambda j, *_: (0, j)),
            scratch_shapes=[
                pltpu.VMEM((tall, shards * stage.wide * BLOCK), b_halves[0].dtype),
                pltpu.SemaphoreType.DMA,
                pltpu.VMEM((tall, tile), jnp.float32),
            ],
        ),
        out_shape=jax.ShapeDtypeStruct((high, sum(widths)), jnp.int16 if pieces else jnp.float32),
        compiler_params=pltpu.CompilerParams(vmem_limit_bytes=VMEM_LIMIT),
        cost_estimate=SMALL,
        name="multiply",
    )(notes, hops, *operands)


def per_device(sizes, a_tiles, a_occupancy, b_tiles, b_occupancy):
    rows, cols, layers = sizes
    me_row, me_col, me_layer = (lax.axis_index(axis).astype(jnp.int32) for axis in ("row", "col", "layer"))
    a_rows, a_k = a_occupancy.shape
    b_k, b_columns = b_occupancy.shape
    piece = a_rows // layers
    given = a_rows - piece
    turn = me_layer.reshape(1)

    def a_place(stage, u, layer):
        row, k = stage.row + u // stage.wide, stage.first + u % stage.wide
        return lax.rem(row + (layer + 1) * piece, a_rows), k

    def b_place(stage, u, _):
        return stage.first + u % stage.wide, stage.row + u // stage.wide

    early = a_k * 3 // 4
    a_stages = [Stage(0, given, 0, a_k), Stage(given, piece, 0, early), Stage(given, piece, early, a_k - early)]
    half = b_columns // 2
    b_stages = [Stage(0, half, 0, b_k), Stage(half, b_columns - half, 0, b_k)]
    a_ends, b_cuts = cuts_for(a_stages, 1.77), cuts_for(b_stages, 2.0)
    a_cuts = sorted({0, max(a_ends[1] // 14, 1), *a_ends})
    a_counts = [a_cuts.index(end) for end in a_ends[1:]]

    a_parts, _ = pack(a_tiles, a_occupancy, turn, a_place, a_stages, a_ends, a_cuts, b_occupancy, (b_place, b_stages, b_cuts))
    heads = [a_parts[0]]
    for hop in range(1, cols):
        heads.append(lax.ppermute(a_parts[0], "col", [(c, (c + hop) % cols) for c in range(cols)]))
    a_parts = [lax.all_gather(part, "col", axis=0) for part in a_parts[1:]]
    b_parts, b_whole = pack(b_tiles, b_occupancy, turn, b_place, b_stages, b_cuts, b_cuts, b_occupancy, None)
    b_first, b_whole = after([b_parts[0], b_whole], heads[1:])
    a_parts = [jnp.stack(heads), *a_parts]

    notes = a_parts[0][:, 0, 0].astype(jnp.int32)
    places_of = lax.rem(me_col - jnp.arange(cols, dtype=jnp.int32) + cols, cols)
    over = jnp.max(a_parts[0][:, 0, :8, MARKS:].astype(jnp.float32), axis=0)[:, OVER - MARKS :]
    over = jnp.broadcast_to(over, (8, BLOCK))

    pair = 2 if rows % 2 == 0 else 1
    swap = [(r, r ^ 1) for r in range(rows)]
    hops = range(1, rows // pair)
    shards = [lax.rem(me_row - pair * hop + rows, rows) for hop in range(rows // pair)]
    b_dense = [None] * len(b_stages)

    def across(part, hop):
        return lax.ppermute(part, "row", [(r, (r + pair * hop) % rows) for r in range(rows)])

    def unpack(h, shard, parts, cuts, *tokens):
        stage = b_stages[h]
        flags = parts[0][0, :b_k, :b_columns].astype(jnp.int32)
        b_dense[h], token = unpack_b(
            parts, flags, shard.reshape(1), rows, stage.row, stage.row + stage.rows, b_k, cuts, b_dense[h], tokens
        )
        return token

    came = [across(b_first, hop) for hop in hops]
    cut = [0, b_cuts[-1]]
    token = turn
    for h in range(2):
        token = unpack(h, shards[0], [b_whole], cut, token)
    if pair == 2:
        other = lax.ppermute(b_whole, "row", swap)
        over = jnp.maximum(over, lax.ppermute(over, "row", swap))
        for h in range(2):
            token = unpack(h, shards[0] ^ 1, [other], cut, token, *[over] * h)

    step = pair
    (over,) = after([over], [token])
    while step < rows:
        over = jnp.maximum(over, lax.ppermute(over, "row", [(r, r ^ step) for r in range(rows)]))
        step *= 2
    *came, b_second = after([*came, b_parts[1]], [token, over])
    sides = [[part] for part in came]
    if pair == 2:
        sides += [[lax.ppermute(part, "row", swap)] for part in came]
    came = [across(b_second, hop) for hop in hops]
    places = [shards[hop] ^ side for side in range(pair) for hop in hops]
    for place, parts in zip(places, sides):
        token = unpack(0, place, parts, b_cuts[:2], token)
    def product_of(g, halves, over, **more):
        return multiply(
            a_parts, notes, places_of, a_stages[: g + 1], a_k, a_cuts[: a_counts[g] + 1], halves, over, **more
        )

    def exchange(codes):
        out, high = [], codes.shape[0] // (layers - 1)
        for q in range(layers - 1):
            there = [(i, (i + 1 + q) % layers) for i in range(layers)]
            out.append(lax.ppermute(codes[q * high : (q + 1) * high], "layer", there))
        return out

    codes = product_of(0, b_dense[:1], over, pieces=layers - 1, remarks=32, tokens=[token])

    came = after(came, [codes])
    first = exchange(codes)
    more = [*came]
    if pair == 2:
        more += [lax.ppermute(part, "row", swap) for part in came]
    for place, parts, part in zip(places, sides, more):
        token = unpack(1, place, [*parts, part], b_cuts, token)
    codes = product_of(0, b_dense[1:], over, pieces=layers - 1, tokens=[token])

    second = exchange(codes)
    product = product_of(1, b_dense, over, tokens=[codes])

    received = [*zip(first, second)]
    product = product_of(2, b_dense, over, received=received, before=(product,))
    over = over[0, 0]
    for codes in second:
        over = jnp.maximum(over, codes[-1, 0].astype(jnp.float32))
    return lax.cond(
        over > 0,
        lambda: whole_slab(sizes, a_tiles, a_occupancy, b_tiles, b_occupancy),
        lambda: product,
    )


def solution(mesh):
    sizes = tuple(mesh.shape[axis] for axis in ("row", "col", "layer"))
    in_specs = (
        P("row", ("layer", "col")),
        P("row", ("layer", "col")),
        P(("layer", "row"), "col"),
        P(("layer", "row"), "col"),
    )
    out_specs = P(("row", "layer"), "col")
    return jax.shard_map(
        functools.partial(per_device, sizes), mesh=mesh, in_specs=in_specs, out_specs=out_specs, check_vma=False
    )
```

```python
import functools
import math
import typing

import jax
import jax.numpy as jnp
from jax import lax
from jax.experimental import pallas as pl
from jax.experimental.pallas import tpu as pltpu
from jax.sharding import PartitionSpec as P

BLOCK = 128
VMEM_LIMIT = 63 * 1024 * 1024
TILE_ROOM = 256 * 16
SMALL = pl.CostEstimate(flops=1, bytes_accessed=1, transcendentals=0)
LARGE = pl.CostEstimate(flops=10**12, bytes_accessed=1, transcendentals=0)


def keep_blocks(values, occupancy):
    height, breadth = values.shape
    tiled = values.reshape(height // BLOCK, BLOCK, breadth // BLOCK, BLOCK)
    flags = occupancy.astype(values.dtype)
    return (tiled * flags[:, None, :, None]).reshape(height, breadth)


def along(part, axis, size, dim):
    me, length = lax.axis_index(axis), part.shape[dim]
    shape = list(part.shape)
    shape[dim] *= size
    whole = lax.dynamic_update_slice_in_dim(jnp.zeros(shape, part.dtype), part, me * length, dim)
    for hop in range(1, size):
        came = lax.ppermute(part, axis, [(i, (i + hop) % size) for i in range(size)])
        whole = lax.dynamic_update_slice_in_dim(whole, came, (me - hop + size) % size * length, dim)
    return whole


def whole_slab(sizes, a_tiles, a_occupancy, b_tiles, b_occupancy):
    rows, cols, layers = sizes
    a_slab = along(keep_blocks(a_tiles, a_occupancy), "col", cols, 1)
    b_kept = keep_blocks(b_tiles, b_occupancy)
    partial_value = jnp.zeros((a_slab.shape[0], b_kept.shape[1]), jnp.float32)
    for hop in range(rows):
        part = lax.ppermute(b_kept, "row", [(i, (i + hop) % rows) for i in range(rows)]) if hop else b_kept
        at = (lax.axis_index("row") - hop + rows) % rows * part.shape[0]
        beside = lax.dynamic_slice_in_dim(a_slab, at, part.shape[0], 1)
        partial_value += jnp.dot(beside, part, preferred_element_type=jnp.float32)
        partial_value, b_kept = lax.optimization_barrier((partial_value, b_kept))
    me, length = lax.axis_index("layer"), partial_value.shape[0] // layers
    total = lax.dynamic_slice_in_dim(partial_value, me * length, length)
    for hop in range(1, layers):
        given = lax.dynamic_slice_in_dim(partial_value, (me + hop) % layers * length, length)
        total += lax.ppermute(given, "layer", [(i, (i + hop) % layers) for i in range(layers)])
    return total


def slots_for(blocks, spread):
    if blocks < 16:
        return blocks + 1
    room = (blocks * 7 + 15) // 16 + int(round(spread * blocks**0.5))
    return min(blocks, room) + 1


def cuts_for(stages, spread):
    cuts, blocks = [0], 0
    for stage in stages:
        blocks += stage.rows * stage.wide
        cuts.append(max(slots_for(blocks, spread), cuts[-1] + 1))
    return cuts


class Stage(typing.NamedTuple):
    row: int
    rows: int
    first: int
    wide: int


def header_of(occupancy):
    rows, columns = occupancy.shape
    flags = occupancy.astype(jnp.bfloat16)
    return jnp.pad(flags, ((0, BLOCK - rows), (0, BLOCK - columns)))


MARKS, OVER = BLOCK - 8, BLOCK - 1


def settle(count, most, held, sem):
    some = 1 << (most.bit_length() - 1)
    while some:

        @pl.when(lax.rem(lax.div(count, some), 2) == 1)
        def _(some=some):
            pltpu.make_async_copy(held.at[pl.ds(0, some)], held.at[pl.ds(0, some)], sem).wait()

        some //= 2


def pack_kernel(place, stages, ends, cuts, other, columns, turn_ref, flags_ref, other_ref, header_ref, values_ref, *refs):
    n = len(cuts) - 1
    parts, (whole, held, sem, out_sems) = refs[:n], refs[-4:]
    if other is None:
        pltpu.make_async_copy(header_ref.at[:BLOCK, :BLOCK], held.at[0], sem).start()
    else:
        held[0] = jnp.zeros_like(held[0])
    lane = lax.broadcasted_iota(jnp.int32, (16, BLOCK), 1)

    def step_of(stage):
        def step(u, carry):
            slot, notes = carry
            row, column = place(stage, u, turn_ref[0])
            flag = flags_ref[row, column]

            @pl.when(flag > 0)
            def _():
                pltpu.make_async_copy(
                    values_ref.at[
                        pl.ds(pl.multiple_of(row * BLOCK, BLOCK), BLOCK),
                        pl.ds(pl.multiple_of(column * BLOCK, BLOCK), BLOCK),
                    ],
                    held.at[jnp.minimum(slot, cuts[-1])],
                    sem,
                ).start()

            if other is not None:
                code = (stage.row + u // stage.wide) * columns + stage.first + u % stage.wide
                notes = jnp.where(lane == jnp.where(flag > 0, slot, BLOCK), code.astype(jnp.float32), notes)
            return slot + flag, notes

        return step

    slot, over, marks = jnp.int32(1), jnp.int32(0), []
    notes = jnp.zeros((16, BLOCK), jnp.float32)
    for stage, cut in zip(stages, ends[1:]):
        marks.append(slot)
        slot, notes = lax.fori_loop(0, stage.rows * stage.wide, step_of(stage), (slot, notes), unroll=8)
        over = jnp.maximum(over, jnp.where(slot > cut, 1, 0))
    marks.append(slot)
    if other is not None:
        other_stages, other_ends = other
        present = other_ref[...]
        column = lax.broadcasted_iota(jnp.int32, present.shape, 1)
        for stage, cut in zip(other_stages, other_ends[1:]):
            spent = 1 + jnp.sum(jnp.where(column < stage.row + stage.rows, present, 0))
            over = jnp.maximum(over, jnp.where(spent > cut, 1, 0))

    settle(slot if other is None else slot - 1, sum(stage.rows * stage.wide for stage in stages) + 1, held, sem)
    if other is not None:
        notes = jnp.where(lane >= MARKS, over.astype(jnp.float32), notes)
        for i, mark in enumerate(marks):
            notes = jnp.where(lane == MARKS + i, mark.astype(jnp.float32), notes)
        held[0, :16, :] = notes.astype(held.dtype)
    copies = [
        pltpu.make_async_copy(held.at[pl.ds(lo, hi - lo)], part, out_sems.at[i])
        for i, (part, lo, hi) in enumerate(zip(parts, cuts[:-1], cuts[1:]))
    ]
    if other is None:
        copies.append(pltpu.make_async_copy(held.at[pl.ds(0, cuts[-1])], whole, out_sems.at[n]))
    for copy in copies:
        copy.start()
    for copy in copies:
        copy.wait()


def pack(values, occupancy, turn, place, stages, ends, cuts, other_flags, other):
    n = len(cuts) - 1
    sizes = [hi - lo for lo, hi in zip(cuts[:-1], cuts[1:])] + [cuts[-1] if other is None else 1]
    if other is None:
        header = header_of(occupancy)
    else:
        header = values
        assert cuts[-1] <= MARKS and len(stages) < OVER - MARKS and occupancy.size <= 256
    *parts, whole = pl.pallas_call(
        functools.partial(pack_kernel, place, stages, ends, cuts, other, occupancy.shape[1]),
        grid_spec=pltpu.PrefetchScalarGridSpec(
            num_scalar_prefetch=2,
            grid=(),
            in_specs=[pl.BlockSpec(memory_space=pltpu.VMEM)] + [pl.BlockSpec(memory_space=pl.ANY)] * 2,
            out_specs=[pl.BlockSpec(memory_space=pl.ANY)] * (n + 1),
            scratch_shapes=[
                pltpu.VMEM((max(cuts[-1], 1 << occupancy.size.bit_length()) + 1, BLOCK, BLOCK), values.dtype),
                pltpu.SemaphoreType.DMA,
                pltpu.SemaphoreType.DMA((n + 1,)),
            ],
        ),
        out_shape=[jax.ShapeDtypeStruct((size, BLOCK, BLOCK), values.dtype) for size in sizes],
        compiler_params=pltpu.CompilerParams(vmem_limit_bytes=VMEM_LIMIT),
        cost_estimate=SMALL,
        name="pack",
    )(turn, occupancy, other_flags, header, values)
    return parts, whole


def after(values, others):
    k = len(values)
    whole = pl.BlockSpec(memory_space=pl.ANY)
    return pl.pallas_call(
        lambda *refs: None,
        in_specs=[whole] * (k + len(others)),
        out_specs=[whole] * k,
        out_shape=[jax.ShapeDtypeStruct(value.shape, value.dtype) for value in values],
        input_output_aliases={i: i for i in range(k)},
        cost_estimate=SMALL,
        name="after",
    )(*values, *others)


def load_list(parts, cuts, held, sems):
    return [
        pltpu.make_async_copy(part, held.at[pl.ds(lo, hi - lo)], sems.at[i])
        for i, (part, lo, hi) in enumerate(zip(parts, cuts[:-1], cuts[1:]))
    ]


def unpack_b_kernel(k_blocks, first, stop, cuts, shard_ref, flags_ref, *refs):
    parts, (out_ref, done_ref, held, sems, sem) = refs[: len(cuts) - 1], refs[-5:]
    done_ref[0] = 0
    nothing = cuts[-1]
    copies = load_list(parts, cuts, held, sems)
    for copy in copies:
        copy.start()
    held[nothing] = jnp.zeros_like(held[nothing])

    def flag_of(t):
        return flags_ref[t % k_blocks, t // k_blocks]

    slot = lax.fori_loop(0, first * k_blocks, lambda t, slot: slot + flag_of(t), jnp.int32(1), unroll=8)
    for copy in copies:
        copy.wait()
    base = shard_ref[0] * k_blocks

    def step(t, slot):
        flag = flag_of(first * k_blocks + t)
        pltpu.make_async_copy(
            held.at[jnp.where(flag > 0, jnp.minimum(slot, nothing), nothing)],
            out_ref.at[
                pl.ds(pl.multiple_of((base + t % k_blocks) * BLOCK, BLOCK), BLOCK),
                pl.ds(pl.multiple_of(t // k_blocks * BLOCK, BLOCK), BLOCK),
            ],
            sem,
        ).start()
        return slot + flag

    lax.fori_loop(0, (stop - first) * k_blocks, step, slot, unroll=8)
    written = out_ref.at[pl.ds(pl.multiple_of(base * BLOCK, BLOCK), k_blocks * BLOCK)]
    pltpu.make_async_copy(written, written, sem).wait()


def unpack_b(parts, flags, shard, shards, first, stop, k_blocks, cuts, into, tokens):
    n = len(parts)
    operands = [*parts, *tokens] + ([] if into is None else [into])
    return pl.pallas_call(
        functools.partial(unpack_b_kernel, k_blocks, first, stop, cuts),
        grid_spec=pltpu.PrefetchScalarGridSpec(
            num_scalar_prefetch=2,
            grid=(),
            in_specs=[pl.BlockSpec(memory_space=pl.ANY)] * len(operands),
            out_specs=[pl.BlockSpec(memory_space=pl.ANY), pl.BlockSpec(memory_space=pltpu.SMEM)],
            scratch_shapes=[
                pltpu.VMEM((cuts[-1] + 1, BLOCK, BLOCK), parts[0].dtype),
                pltpu.SemaphoreType.DMA((n,)),
                pltpu.SemaphoreType.DMA,
            ],
        ),
        out_shape=[
            jax.ShapeDtypeStruct((shards * k_blocks * BLOCK, (stop - first) * BLOCK), parts[0].dtype),
            jax.ShapeDtypeStruct((1,), jnp.int32),
        ],
        input_output_aliases={} if into is None else {2 + n + len(tokens): 0},
        compiler_params=pltpu.CompilerParams(vmem_limit_bytes=VMEM_LIMIT),
        cost_estimate=SMALL,
        name="unpack_b",
    )(shard, flags, *operands)


def multiply_kernel(plan, notes_ref, hop_ref, *refs):
    stages, k_blocks, cuts, shards, halves, given, carried, tokens, pieces, remarks, starts, ends, by_hop = plan
    stage, g = stages[-1], len(stages) - 1
    rows, wide = stage.rows, stage.wide
    n = len(cuts) - 1
    parts, refs = refs[:n], refs[n:]
    b_refs, refs = refs[:halves], refs[halves:]
    codes_in, refs = refs[: halves * given], refs[halves * given :]
    before, refs = refs[:carried], refs[carried + tokens :]
    over_ref, out_ref, *word_ref, dense, sem, total = refs

    def fill():
        dense[...] = jnp.zeros_like(dense)
        started = jnp.int32(0)
        for s in range(shards):
            base, hop = s * wide - stage.first, hop_ref[s]

            for i, (part, lo, hi) in enumerate(zip(parts, cuts[:-1], cuts[1:])):
                at = hop if i in by_hop else s


                def put(slot, _):
                    code = notes_ref[hop, slot]
                    row, k = lax.div(code, k_blocks), lax.rem(code, k_blocks)
                    pltpu.make_async_copy(
                        part.at[at, slot - lo],
                        dense.at[
                            pl.ds(pl.multiple_of((row - stage.row) * BLOCK, BLOCK), BLOCK),
                            pl.ds(pl.multiple_of((base + k) * BLOCK, BLOCK), BLOCK),
                        ],
                        sem,
                    ).start()
                    return 0

                first = jnp.maximum(notes_ref[hop, MARKS + g], lo)
                stop = jnp.maximum(jnp.minimum(notes_ref[hop, MARKS + g + 1], hi), first)
                lax.fori_loop(first, stop, put, 0)
                started += stop - first

        def settle(t, _):
            pltpu.make_async_copy(parts[0].at[0, 0], dense.at[:BLOCK, :BLOCK], sem).wait()
            return 0

        lax.fori_loop(0, started, settle, 0)

    pl.when(pl.program_id(0) == 0)(fill)

    def code(here):
        share = rows // pieces
        for q in range(pieces):
            base = q * (share * BLOCK + remarks)
            powers = []
            for r in range(share):
                some = total[(q * share + r) * BLOCK : (q * share + r + 1) * BLOCK, here]
                top = jnp.max(jnp.abs(some), axis=0, keepdims=True)
                power = jnp.clip(jnp.ceil(jnp.log2(top)), -60.0, 60.0)
                some = jnp.clip(jnp.round(some * jnp.exp2(15.0 - power)), -32767.0, 32767.0)
                out_ref[base + r * BLOCK : base + (r + 1) * BLOCK, here] = some.astype(jnp.int32).astype(jnp.int16)
                powers.append(power)
            flag = jnp.broadcast_to(over_ref[0:1, 0:1], powers[0].shape)
            notes = jnp.concatenate(powers + [flag] * (remarks - share), axis=0)
            out_ref[base + share * BLOCK : base + share * BLOCK + remarks, here] = notes.astype(jnp.int32).astype(jnp.int16)

    def finish(here, h):
        for r in range(rows):
            span = slice(r * BLOCK, (r + 1) * BLOCK)
            some = total[span, here]
            for q in range(given):
                codes = codes_in[q * halves + h]
                notes = codes[rows * BLOCK : rows * BLOCK + 16, here].astype(jnp.int32).astype(jnp.float32)
                some += codes[span, here].astype(jnp.int32).astype(jnp.float32) * jnp.exp2(notes[r : r + 1] - 15.0)
            for earlier in before:
                some += earlier[span, here]
            out_ref[span, here] = some
        if given and h == halves - 1:
            over = jnp.max(over_ref[...])
            for q in range(given):
                remarks = codes_in[q * halves + h][-16:, :BLOCK].astype(jnp.int32).astype(jnp.float32)
                over = jnp.maximum(over, jnp.max(remarks[15:]))
            word_ref[0][0] = over.astype(jnp.int32)

    for h, b_ref in enumerate(b_refs):

        @pl.when((pl.program_id(0) >= starts[h]) & (pl.program_id(0) < ends[h]))
        def _():
            span = min(b_ref.shape[-1], 256)
            for at in range(0, b_ref.shape[-1], span):
                here = slice(at, at + span)
                b_here = b_ref[..., here].reshape(-1, span)
                total[:, here] = jnp.dot(dense[...], b_here, preferred_element_type=jnp.float32)
                if pieces:
                    code(here)
                else:
                    finish(here, h)


def multiply(
    parts, notes, hops, by_hop, stages, k_blocks, cuts, b_halves, over, pieces=0, remarks=16, received=(), before=(), tokens=()
):
    shards, halves = parts[0].shape[0], len(b_halves)
    stage = stages[-1]
    n = len(cuts) - 1
    widths = [b_half.shape[1] for b_half in b_halves]
    shared = math.gcd(*widths)
    tile = max(t for t in (BLOCK, 256, 512) if shared % t == 0 and t * stage.wide <= TILE_ROOM)
    ends = [sum(widths[: h + 1]) // tile for h in range(halves)]
    starts = [0] + ends[:-1]
    deep = math.gcd(math.gcd(stage.first, stage.wide), k_blocks)
    layers, skip = stage.wide // deep, stage.first // deep
    assert skip % layers == 0
    tall = stage.rows * BLOCK
    whole = pl.BlockSpec(memory_space=pl.ANY)

    def at(h, *fixed):
        return lambda j, *_: (*fixed, jnp.clip(j - starts[h], 0, ends[h] - starts[h] - 1))

    in_specs = [whole] * n
    operands = [*parts[:n]]
    for h, b_half in enumerate(b_halves):
        in_specs.append(pl.BlockSpec((shards, layers, deep * BLOCK, tile), at(h, 0, skip // layers, 0)))
        operands.append(b_half.reshape(shards, k_blocks // deep, deep * BLOCK, widths[h]))
    for pairs in received:
        for h, codes in enumerate(pairs):
            in_specs.append(pl.BlockSpec((codes.shape[0], tile), at(h, 0)))
            operands.append(codes)
    in_specs += [pl.BlockSpec((tall, tile), lambda j, *_: (0, j))] * len(before)
    operands += [*before]
    in_specs += [whole] * len(tokens) + [pl.BlockSpec(memory_space=pltpu.VMEM)]
    operands += [*tokens, over]
    high = tall + remarks * pieces
    out_specs = [pl.BlockSpec((high, tile), lambda j, *_: (0, j))]
    out_shape = [jax.ShapeDtypeStruct((high, sum(widths)), jnp.int16 if pieces else jnp.float32)]
    if received:
        out_specs.append(pl.BlockSpec(memory_space=pltpu.SMEM))
        out_shape.append(jax.ShapeDtypeStruct((1,), jnp.int32))
    plan = (stages, k_blocks, cuts, shards, halves, len(received), len(before), len(tokens), pieces, remarks, starts, ends, by_hop)
    return pl.pallas_call(
        functools.partial(multiply_kernel, plan),
        grid_spec=pltpu.PrefetchScalarGridSpec(
            num_scalar_prefetch=2,
            grid=(ends[-1],),
            in_specs=in_specs,
            out_specs=out_specs,
            scratch_shapes=[
                pltpu.VMEM((tall, shards * stage.wide * BLOCK), b_halves[0].dtype),
                pltpu.SemaphoreType.DMA,
                pltpu.VMEM((tall, tile), jnp.float32),
            ],
        ),
        out_shape=out_shape,
        compiler_params=pltpu.CompilerParams(vmem_limit_bytes=VMEM_LIMIT),
        cost_estimate=SMALL,
        name="multiply",
    )(notes, hops, *operands)


def per_device(sizes, a_tiles, a_occupancy, b_tiles, b_occupancy):
    rows, cols, layers = sizes
    me_row, me_col, me_layer = (lax.axis_index(axis).astype(jnp.int32) for axis in ("row", "col", "layer"))
    a_rows, a_k = a_occupancy.shape
    b_k, b_columns = b_occupancy.shape
    piece = a_rows // layers
    given = a_rows - piece
    turn = me_layer.reshape(1)

    def a_place(stage, u, layer):
        row, k = stage.row + u // stage.wide, stage.first + u % stage.wide
        return lax.rem(row + (layer + 1) * piece, a_rows), k

    def b_place(stage, u, _):
        return stage.first + u % stage.wide, stage.row + u // stage.wide

    early = a_k * 3 // 4
    a_stages = [Stage(0, given, 0, a_k), Stage(given, piece, 0, early), Stage(given, piece, early, a_k - early)]
    half = b_columns // 2
    b_stages = [Stage(0, half, 0, b_k), Stage(half, b_columns - half, 0, b_k)]
    a_ends, b_cuts = cuts_for(a_stages, 1.77), cuts_for(b_stages, 2.0)
    a_cuts = sorted({0, max(a_ends[1] // 14, 1), a_ends[1] + max((a_ends[2] - a_ends[1]) // 6, 1), *a_ends})
    assert len(a_cuts) == 6
    a_counts = [a_cuts.index(end) for end in a_ends[1:]]

    a_parts, _ = pack(a_tiles, a_occupancy, turn, a_place, a_stages, a_ends, a_cuts, b_occupancy, (b_stages, b_cuts))
    def round_col(part):
        return [part] + [lax.ppermute(part, "col", [(c, (c + hop) % cols) for c in range(cols)]) for hop in range(1, cols)]

    heads = round_col(a_parts[0])
    more_a = a_parts[2]
    a_parts = [None if i in (0, 2) else lax.all_gather(part, "col", axis=0) for i, part in enumerate(a_parts)]
    b_parts, b_whole = pack(b_tiles, b_occupancy, turn, b_place, b_stages, b_cuts, b_cuts, b_occupancy, None)
    b_first, b_whole = after([b_parts[0], b_whole], heads[1:])
    a_parts[0] = jnp.stack(heads)

    notes = a_parts[0][:, 0, 0].astype(jnp.int32)
    places_of = lax.rem(me_col - jnp.arange(cols, dtype=jnp.int32) + cols, cols)
    over = jnp.max(a_parts[0][:, 0, :8, MARKS:].astype(jnp.float32), axis=0)[:, OVER - MARKS :]
    over = jnp.broadcast_to(over, (8, BLOCK))

    pair = 2 if rows % 2 == 0 else 1
    swap = [(r, r ^ 1) for r in range(rows)]
    hops = range(1, rows // pair)
    shards = [lax.rem(me_row - pair * hop + rows, rows) for hop in range(rows // pair)]
    b_dense = [None] * len(b_stages)

    def across(part, hop):
        return lax.ppermute(part, "row", [(r, (r + pair * hop) % rows) for r in range(rows)])

    def unpack(h, shard, parts, cuts, *tokens):
        stage = b_stages[h]
        flags = parts[0][0, :b_k, :b_columns].astype(jnp.int32)
        b_dense[h], token = unpack_b(
            parts, flags, shard.reshape(1), rows, stage.row, stage.row + stage.rows, b_k, cuts, b_dense[h], tokens
        )
        return token

    came = [across(b_first, hop) for hop in hops]
    cut = [0, b_cuts[-1]]
    token = turn
    for h in range(2):
        token = unpack(h, shards[0], [b_whole], cut, token)
    if pair == 2:
        other = lax.ppermute(b_whole, "row", swap)
        over = jnp.maximum(over, lax.ppermute(over, "row", swap))
        for h in range(2):
            token = unpack(h, shards[0] ^ 1, [other], cut, token, *[over] * h)

    step = pair
    (over,) = after([over], [token])
    while step < rows:
        over = jnp.maximum(over, lax.ppermute(over, "row", [(r, r ^ step) for r in range(rows)]))
        step *= 2
    *came, b_second = after([*came, b_parts[1]], [token, over])
    sides = [[part] for part in came]
    if pair == 2:
        sides += [[lax.ppermute(part, "row", swap)] for part in came]
    came = [across(b_second, hop) for hop in hops]
    places = [shards[hop] ^ side for side in range(pair) for hop in hops]
    for place, parts in zip(places, sides):
        token = unpack(0, place, parts, b_cuts[:2], token)
    def product_of(g, halves, over, **more):
        return multiply(
            a_parts, notes, places_of, (0, 2), a_stages[: g + 1], a_k, a_cuts[: a_counts[g] + 1], halves, over, **more
        )

    def exchange(codes):
        out, high = [], codes.shape[0] // (layers - 1)
        for q in range(layers - 1):
            there = [(i, (i + 1 + q) % layers) for i in range(layers)]
            out.append(lax.ppermute(codes[q * high : (q + 1) * high], "layer", there))
        return out

    (more_a,) = after([more_a], [token, a_parts[1]])
    more_a = round_col(more_a)
    (codes,) = product_of(0, b_dense[:1], over, pieces=layers - 1, remarks=32, tokens=[token])

    came = after(came, [codes, *more_a[1:]])
    a_parts[2] = jnp.stack(more_a)
    first = exchange(codes)
    more = [*came]
    if pair == 2:
        more += [lax.ppermute(part, "row", swap) for part in came]
    for place, parts, part in zip(places, sides, more):
        token = unpack(1, place, [*parts, part], b_cuts, token)
    (codes,) = product_of(0, b_dense[1:], over, pieces=layers - 1, tokens=[token])

    second = exchange(codes)
    (product,) = product_of(1, b_dense, over, tokens=[codes])

    received = [*zip(first, second)]
    product, over = product_of(2, b_dense, over, received=received, before=(product,))
    return lax.cond(
        over[0] > 0,
        lambda: whole_slab(sizes, a_tiles, a_occupancy, b_tiles, b_occupancy),
        lambda: product,
    )


def solution(mesh):
    sizes = tuple(mesh.shape[axis] for axis in ("row", "col", "layer"))
    in_specs = (
        P("row", ("layer", "col")),
        P("row", ("layer", "col")),
        P(("layer", "row"), "col"),
        P(("layer", "row"), "col"),
    )
    out_specs = P(("row", "layer"), "col")
    return jax.shard_map(
        functools.partial(per_device, sizes), mesh=mesh, in_specs=in_specs, out_specs=out_specs, check_vma=False
    )
```

```python
import functools
import math
import typing

import jax
import jax.numpy as jnp
from jax import lax
from jax.experimental import pallas as pl
from jax.experimental.pallas import tpu as pltpu
from jax.sharding import PartitionSpec as P

BLOCK = 128
VMEM_LIMIT = 63 * 1024 * 1024
TILE_ROOM = 256 * 16
SMALL = pl.CostEstimate(flops=1, bytes_accessed=1, transcendentals=0)
LARGE = pl.CostEstimate(flops=10**12, bytes_accessed=1, transcendentals=0)


def keep_blocks(values, occupancy):
    height, breadth = values.shape
    tiled = values.reshape(height // BLOCK, BLOCK, breadth // BLOCK, BLOCK)
    flags = occupancy.astype(values.dtype)
    return (tiled * flags[:, None, :, None]).reshape(height, breadth)


def along(part, axis, size, dim):
    me, length = lax.axis_index(axis), part.shape[dim]
    shape = list(part.shape)
    shape[dim] *= size
    whole = lax.dynamic_update_slice_in_dim(jnp.zeros(shape, part.dtype), part, me * length, dim)
    for hop in range(1, size):
        came = lax.ppermute(part, axis, [(i, (i + hop) % size) for i in range(size)])
        whole = lax.dynamic_update_slice_in_dim(whole, came, (me - hop + size) % size * length, dim)
    return whole


def whole_slab(sizes, a_tiles, a_occupancy, b_tiles, b_occupancy):
    rows, cols, layers = sizes
    a_slab = along(keep_blocks(a_tiles, a_occupancy), "col", cols, 1)
    b_kept = keep_blocks(b_tiles, b_occupancy)
    partial_value = jnp.zeros((a_slab.shape[0], b_kept.shape[1]), jnp.float32)
    for hop in range(rows):
        part = lax.ppermute(b_kept, "row", [(i, (i + hop) % rows) for i in range(rows)]) if hop else b_kept
        at = (lax.axis_index("row") - hop + rows) % rows * part.shape[0]
        beside = lax.dynamic_slice_in_dim(a_slab, at, part.shape[0], 1)
        partial_value += jnp.dot(beside, part, preferred_element_type=jnp.float32)
        partial_value, b_kept = lax.optimization_barrier((partial_value, b_kept))
    me, length = lax.axis_index("layer"), partial_value.shape[0] // layers
    total = lax.dynamic_slice_in_dim(partial_value, me * length, length)
    for hop in range(1, layers):
        given = lax.dynamic_slice_in_dim(partial_value, (me + hop) % layers * length, length)
        total += lax.ppermute(given, "layer", [(i, (i + hop) % layers) for i in range(layers)])
    return total


def slots_for(blocks, spread):
    if blocks < 16:
        return blocks + 1
    room = (blocks * 7 + 15) // 16 + int(round(spread * blocks**0.5))
    return min(blocks, room) + 1


def cuts_for(stages, spread):
    cuts, blocks = [0], 0
    for stage in stages:
        blocks += stage.rows * stage.wide
        cuts.append(max(slots_for(blocks, spread), cuts[-1] + 1))
    return cuts


class Stage(typing.NamedTuple):
    row: int
    rows: int
    first: int
    wide: int


def header_of(occupancy):
    rows, columns = occupancy.shape
    flags = occupancy.astype(jnp.bfloat16)
    return jnp.pad(flags, ((0, BLOCK - rows), (0, BLOCK - columns)))


MARKS, OVER = BLOCK - 8, BLOCK - 1


def settle(count, most, held, sem):
    some = 1 << (most.bit_length() - 1)
    while some:

        @pl.when(lax.rem(lax.div(count, some), 2) == 1)
        def _(some=some):
            pltpu.make_async_copy(held.at[pl.ds(0, some)], held.at[pl.ds(0, some)], sem).wait()

        some //= 2


def pack_kernel(place, stages, ends, cuts, other, columns, turn_ref, flags_ref, other_ref, header_ref, values_ref, *refs):
    n = len(cuts) - 1
    parts, (whole, held, sem, out_sems) = refs[:n], refs[-4:]
    if other is None:
        pltpu.make_async_copy(header_ref.at[:BLOCK, :BLOCK], held.at[0], sem).start()
    else:
        held[0] = jnp.zeros_like(held[0])
    lane = lax.broadcasted_iota(jnp.int32, (16, BLOCK), 1)

    def step_of(stage):
        def step(u, carry):
            slot, notes = carry
            row, column = place(stage, u, turn_ref[0])
            flag = flags_ref[row, column]

            @pl.when(flag > 0)
            def _():
                pltpu.make_async_copy(
                    values_ref.at[
                        pl.ds(pl.multiple_of(row * BLOCK, BLOCK), BLOCK),
                        pl.ds(pl.multiple_of(column * BLOCK, BLOCK), BLOCK),
                    ],
                    held.at[jnp.minimum(slot, cuts[-1])],
                    sem,
                ).start()

            if other is not None:
                code = (stage.row + u // stage.wide) * columns + stage.first + u % stage.wide
                notes = jnp.where(lane == jnp.where(flag > 0, slot, BLOCK), code.astype(jnp.float32), notes)
            return slot + flag, notes

        return step

    slot, over, marks = jnp.int32(1), jnp.int32(0), []
    notes = jnp.zeros((16, BLOCK), jnp.float32)
    for stage, cut in zip(stages, ends[1:]):
        marks.append(slot)
        slot, notes = lax.fori_loop(0, stage.rows * stage.wide, step_of(stage), (slot, notes), unroll=8)
        over = jnp.maximum(over, jnp.where(slot > cut, 1, 0))
    marks.append(slot)
    if other is not None:
        other_stages, other_ends = other
        present = other_ref[...]
        column = lax.broadcasted_iota(jnp.int32, present.shape, 1)
        for stage, cut in zip(other_stages, other_ends[1:]):
            spent = 1 + jnp.sum(jnp.where(column < stage.row + stage.rows, present, 0))
            over = jnp.maximum(over, jnp.where(spent > cut, 1, 0))

    settle(slot if other is None else slot - 1, sum(stage.rows * stage.wide for stage in stages) + 1, held, sem)
    if other is not None:
        notes = jnp.where(lane >= MARKS, over.astype(jnp.float32), notes)
        for i, mark in enumerate(marks):
            notes = jnp.where(lane == MARKS + i, mark.astype(jnp.float32), notes)
        held[0, :16, :] = notes.astype(held.dtype)
    copies = [
        pltpu.make_async_copy(held.at[pl.ds(lo, hi - lo)], part, out_sems.at[i])
        for i, (part, lo, hi) in enumerate(zip(parts, cuts[:-1], cuts[1:]))
    ]
    if other is None:
        copies.append(pltpu.make_async_copy(held.at[pl.ds(0, cuts[-1])], whole, out_sems.at[n]))
    for copy in copies:
        copy.start()
    for copy in copies:
        copy.wait()


def pack(values, occupancy, turn, place, stages, ends, cuts, other_flags, other):
    n = len(cuts) - 1
    sizes = [hi - lo for lo, hi in zip(cuts[:-1], cuts[1:])] + [cuts[-1] if other is None else 1]
    if other is None:
        header = header_of(occupancy)
    else:
        header = values
        assert cuts[-1] <= MARKS and len(stages) < OVER - MARKS and occupancy.size <= 256
    *parts, whole = pl.pallas_call(
        functools.partial(pack_kernel, place, stages, ends, cuts, other, occupancy.shape[1]),
        grid_spec=pltpu.PrefetchScalarGridSpec(
            num_scalar_prefetch=2,
            grid=(),
            in_specs=[pl.BlockSpec(memory_space=pltpu.VMEM)] + [pl.BlockSpec(memory_space=pl.ANY)] * 2,
            out_specs=[pl.BlockSpec(memory_space=pl.ANY)] * (n + 1),
            scratch_shapes=[
                pltpu.VMEM((max(cuts[-1], 1 << occupancy.size.bit_length()) + 1, BLOCK, BLOCK), values.dtype),
                pltpu.SemaphoreType.DMA,
                pltpu.SemaphoreType.DMA((n + 1,)),
            ],
        ),
        out_shape=[jax.ShapeDtypeStruct((size, BLOCK, BLOCK), values.dtype) for size in sizes],
        compiler_params=pltpu.CompilerParams(vmem_limit_bytes=VMEM_LIMIT),
        cost_estimate=SMALL,
        name="pack",
    )(turn, occupancy, other_flags, header, values)
    return parts, whole


def after(values, others):
    k = len(values)
    whole = pl.BlockSpec(memory_space=pl.ANY)
    return pl.pallas_call(
        lambda *refs: None,
        in_specs=[whole] * (k + len(others)),
        out_specs=[whole] * k,
        out_shape=[jax.ShapeDtypeStruct(value.shape, value.dtype) for value in values],
        input_output_aliases={i: i for i in range(k)},
        cost_estimate=SMALL,
        name="after",
    )(*values, *others)


def load_list(parts, cuts, held, sems):
    return [
        pltpu.make_async_copy(part, held.at[pl.ds(lo, hi - lo)], sems.at[i])
        for i, (part, lo, hi) in enumerate(zip(parts, cuts[:-1], cuts[1:]))
    ]


def unpack_b_kernel(k_blocks, first, stop, cuts, shard_ref, flags_ref, *refs):
    parts, (out_ref, done_ref, held, sems, sem) = refs[: len(cuts) - 1], refs[-5:]
    done_ref[0] = 0
    nothing = cuts[-1]
    copies = load_list(parts, cuts, held, sems)
    for copy in copies:
        copy.start()
    held[nothing] = jnp.zeros_like(held[nothing])

    def flag_of(t):
        return flags_ref[t % k_blocks, t // k_blocks]

    slot = lax.fori_loop(0, first * k_blocks, lambda t, slot: slot + flag_of(t), jnp.int32(1), unroll=8)
    for copy in copies:
        copy.wait()
    base = shard_ref[0] * k_blocks

    def step(t, slot):
        flag = flag_of(first * k_blocks + t)
        pltpu.make_async_copy(
            held.at[jnp.where(flag > 0, jnp.minimum(slot, nothing), nothing)],
            out_ref.at[
                pl.ds(pl.multiple_of((base + t % k_blocks) * BLOCK, BLOCK), BLOCK),
                pl.ds(pl.multiple_of(t // k_blocks * BLOCK, BLOCK), BLOCK),
            ],
            sem,
        ).start()
        return slot + flag

    lax.fori_loop(0, (stop - first) * k_blocks, step, slot, unroll=8)
    written = out_ref.at[pl.ds(pl.multiple_of(base * BLOCK, BLOCK), k_blocks * BLOCK)]
    pltpu.make_async_copy(written, written, sem).wait()


def unpack_b(parts, flags, shard, shards, first, stop, k_blocks, cuts, into, tokens):
    n = len(parts)
    operands = [*parts, *tokens] + ([] if into is None else [into])
    return pl.pallas_call(
        functools.partial(unpack_b_kernel, k_blocks, first, stop, cuts),
        grid_spec=pltpu.PrefetchScalarGridSpec(
            num_scalar_prefetch=2,
            grid=(),
            in_specs=[pl.BlockSpec(memory_space=pl.ANY)] * len(operands),
            out_specs=[pl.BlockSpec(memory_space=pl.ANY), pl.BlockSpec(memory_space=pltpu.SMEM)],
            scratch_shapes=[
                pltpu.VMEM((cuts[-1] + 1, BLOCK, BLOCK), parts[0].dtype),
                pltpu.SemaphoreType.DMA((n,)),
                pltpu.SemaphoreType.DMA,
            ],
        ),
        out_shape=[
            jax.ShapeDtypeStruct((shards * k_blocks * BLOCK, (stop - first) * BLOCK), parts[0].dtype),
            jax.ShapeDtypeStruct((1,), jnp.int32),
        ],
        input_output_aliases={} if into is None else {2 + n + len(tokens): 0},
        compiler_params=pltpu.CompilerParams(vmem_limit_bytes=VMEM_LIMIT),
        cost_estimate=SMALL,
        name="unpack_b",
    )(shard, flags, *operands)


def multiply_kernel(plan, notes_ref, hop_ref, *refs):
    stages, k_blocks, cuts, shards, halves, given, carried, tokens, pieces, remarks, starts, ends, by_hop = plan
    stage, g = stages[-1], len(stages) - 1
    rows, wide = stage.rows, stage.wide
    n = len(cuts) - 1
    parts, refs = refs[:n], refs[n:]
    b_refs, refs = refs[:halves], refs[halves:]
    codes_in, refs = refs[: halves * given], refs[halves * given :]
    before, refs = refs[:carried], refs[carried + tokens :]
    over_ref, out_ref, *word_ref, dense, sem, total = refs

    def fill():
        dense[...] = jnp.zeros_like(dense)
        started = jnp.int32(0)
        for s in range(shards):
            base, hop = s * wide - stage.first, hop_ref[s]

            for i, (part, lo, hi) in enumerate(zip(parts, cuts[:-1], cuts[1:])):
                at = hop if i in by_hop else s


                def put(slot, _):
                    code = notes_ref[hop, slot]
                    row, k = lax.div(code, k_blocks), lax.rem(code, k_blocks)
                    pltpu.make_async_copy(
                        part.at[at, slot - lo],
                        dense.at[
                            pl.ds(pl.multiple_of((row - stage.row) * BLOCK, BLOCK), BLOCK),
                            pl.ds(pl.multiple_of((base + k) * BLOCK, BLOCK), BLOCK),
                        ],
                        sem,
                    ).start()
                    return 0

                first = jnp.maximum(notes_ref[hop, MARKS + g], lo)
                stop = jnp.maximum(jnp.minimum(notes_ref[hop, MARKS + g + 1], hi), first)
                lax.fori_loop(first, stop, put, 0)
                started += stop - first

        some = 1 << ((rows * wide * shards).bit_length() - 1)
        while some:
            broad = min(some, 1 << ((wide * shards).bit_length() - 1))
            here = dense.at[: some // broad * BLOCK, : broad * BLOCK]

            @pl.when(lax.rem(lax.div(started, some), 2) == 1)
            def _(here=here):
                pltpu.make_async_copy(here, here, sem).wait()

            some //= 2

    pl.when(pl.program_id(0) == 0)(fill)

    def code(here):
        share = rows // pieces
        for q in range(pieces):
            base = q * (share * BLOCK + remarks)
            powers = []
            for r in range(share):
                some = total[(q * share + r) * BLOCK : (q * share + r + 1) * BLOCK, here]
                top = jnp.max(jnp.abs(some), axis=0, keepdims=True)
                power = jnp.clip(jnp.ceil(jnp.log2(top)), -60.0, 60.0)
                some = jnp.clip(jnp.round(some * jnp.exp2(15.0 - power)), -32767.0, 32767.0)
                out_ref[base + r * BLOCK : base + (r + 1) * BLOCK, here] = some.astype(jnp.int32).astype(jnp.int16)
                powers.append(power)
            flag = jnp.broadcast_to(over_ref[0:1, 0:1], powers[0].shape)
            notes = jnp.concatenate(powers + [flag] * (remarks - share), axis=0)
            out_ref[base + share * BLOCK : base + share * BLOCK + remarks, here] = notes.astype(jnp.int32).astype(jnp.int16)

    def finish(here, h):
        for r in range(rows):
            span = slice(r * BLOCK, (r + 1) * BLOCK)
            some = total[span, here]
            for q in range(given):
                codes = codes_in[q * halves + h]
                notes = codes[rows * BLOCK : rows * BLOCK + 16, here].astype(jnp.int32).astype(jnp.float32)
                some += codes[span, here].astype(jnp.int32).astype(jnp.float32) * jnp.exp2(notes[r : r + 1] - 15.0)
            for earlier in before:
                some += earlier[span, here]
            out_ref[span, here] = some
        if given and h == halves - 1:
            over = jnp.max(over_ref[...])
            for q in range(given):
                remarks = codes_in[q * halves + h][-16:, :BLOCK].astype(jnp.int32).astype(jnp.float32)
                over = jnp.maximum(over, jnp.max(remarks[15:]))
            word_ref[0][0] = over.astype(jnp.int32)

    for h, b_ref in enumerate(b_refs):

        @pl.when((pl.program_id(0) >= starts[h]) & (pl.program_id(0) < ends[h]))
        def _():
            span = min(b_ref.shape[-1], 256)
            for at in range(0, b_ref.shape[-1], span):
                here = slice(at, at + span)
                b_here = b_ref[..., here].reshape(-1, span)
                total[:, here] = jnp.dot(dense[...], b_here, preferred_element_type=jnp.float32)
                if pieces:
                    code(here)
                else:
                    finish(here, h)


def multiply(
    parts, notes, hops, by_hop, stages, k_blocks, cuts, b_halves, over, pieces=0, remarks=16, received=(), before=(), tokens=()
):
    shards, halves = parts[0].shape[0], len(b_halves)
    stage = stages[-1]
    n = len(cuts) - 1
    widths = [b_half.shape[1] for b_half in b_halves]
    shared = math.gcd(*widths)
    tile = max(t for t in (BLOCK, 256, 512) if shared % t == 0 and t * stage.wide <= TILE_ROOM)
    ends = [sum(widths[: h + 1]) // tile for h in range(halves)]
    starts = [0] + ends[:-1]
    deep = math.gcd(math.gcd(stage.first, stage.wide), k_blocks)
    layers, skip = stage.wide // deep, stage.first // deep
    assert skip % layers == 0
    tall = stage.rows * BLOCK
    whole = pl.BlockSpec(memory_space=pl.ANY)

    def at(h, *fixed):
        return lambda j, *_: (*fixed, jnp.clip(j - starts[h], 0, ends[h] - starts[h] - 1))

    in_specs = [whole] * n
    operands = [*parts[:n]]
    for h, b_half in enumerate(b_halves):
        in_specs.append(pl.BlockSpec((shards, layers, deep * BLOCK, tile), at(h, 0, skip // layers, 0)))
        operands.append(b_half.reshape(shards, k_blocks // deep, deep * BLOCK, widths[h]))
    for pairs in received:
        for h, codes in enumerate(pairs):
            in_specs.append(pl.BlockSpec((codes.shape[0], tile), at(h, 0)))
            operands.append(codes)
    in_specs += [pl.BlockSpec((tall, tile), lambda j, *_: (0, j))] * len(before)
    operands += [*before]
    in_specs += [whole] * len(tokens) + [pl.BlockSpec(memory_space=pltpu.VMEM)]
    operands += [*tokens, over]
    high = tall + remarks * pieces
    out_specs = [pl.BlockSpec((high, tile), lambda j, *_: (0, j))]
    out_shape = [jax.ShapeDtypeStruct((high, sum(widths)), jnp.int16 if pieces else jnp.float32)]
    if received:
        out_specs.append(pl.BlockSpec(memory_space=pltpu.SMEM))
        out_shape.append(jax.ShapeDtypeStruct((1,), jnp.int32))
    plan = (stages, k_blocks, cuts, shards, halves, len(received), len(before), len(tokens), pieces, remarks, starts, ends, by_hop)
    return pl.pallas_call(
        functools.partial(multiply_kernel, plan),
        grid_spec=pltpu.PrefetchScalarGridSpec(
            num_scalar_prefetch=2,
            grid=(ends[-1],),
            in_specs=in_specs,
            out_specs=out_specs,
            scratch_shapes=[
                pltpu.VMEM((tall, shards * stage.wide * BLOCK), b_halves[0].dtype),
                pltpu.SemaphoreType.DMA,
                pltpu.VMEM((tall, tile), jnp.float32),
            ],
        ),
        out_shape=out_shape,
        compiler_params=pltpu.CompilerParams(vmem_limit_bytes=VMEM_LIMIT),
        cost_estimate=SMALL,
        name="multiply",
    )(notes, hops, *operands)


def per_device(sizes, a_tiles, a_occupancy, b_tiles, b_occupancy):
    rows, cols, layers = sizes
    me_row, me_col, me_layer = (lax.axis_index(axis).astype(jnp.int32) for axis in ("row", "col", "layer"))
    a_rows, a_k = a_occupancy.shape
    b_k, b_columns = b_occupancy.shape
    piece = a_rows // layers
    given = a_rows - piece
    turn = me_layer.reshape(1)

    def a_place(stage, u, layer):
        row, k = stage.row + u // stage.wide, stage.first + u % stage.wide
        return lax.rem(row + (layer + 1) * piece, a_rows), k

    def b_place(stage, u, _):
        return stage.first + u % stage.wide, stage.row + u // stage.wide

    early = a_k * 3 // 4
    a_stages = [Stage(0, given, 0, a_k), Stage(given, piece, 0, early), Stage(given, piece, early, a_k - early)]
    half = b_columns // 2
    b_stages = [Stage(0, half, 0, b_k), Stage(half, b_columns - half, 0, b_k)]
    a_ends, b_cuts = cuts_for(a_stages, 1.77), cuts_for(b_stages, 2.0)
    a_cuts = sorted({0, max(a_ends[1] // 14, 1), a_ends[1] + max((a_ends[2] - a_ends[1]) // 6, 1), *a_ends})
    assert len(a_cuts) == 6
    a_counts = [a_cuts.index(end) for end in a_ends[1:]]

    a_parts, _ = pack(a_tiles, a_occupancy, turn, a_place, a_stages, a_ends, a_cuts, b_occupancy, (b_stages, b_cuts))
    def round_col(part):
        return [part] + [lax.ppermute(part, "col", [(c, (c + hop) % cols) for c in range(cols)]) for hop in range(1, cols)]

    heads = round_col(a_parts[0])
    more_a = a_parts[2]
    a_parts = [None if i in (0, 2) else lax.all_gather(part, "col", axis=0) for i, part in enumerate(a_parts)]
    b_parts, b_whole = pack(b_tiles, b_occupancy, turn, b_place, b_stages, b_cuts, b_cuts, b_occupancy, None)
    b_first, b_whole = after([b_parts[0], b_whole], heads[1:])
    a_parts[0] = jnp.stack(heads)

    notes = a_parts[0][:, 0, 0].astype(jnp.int32)
    places_of = lax.rem(me_col - jnp.arange(cols, dtype=jnp.int32) + cols, cols)
    over = jnp.max(a_parts[0][:, 0, :8, MARKS:].astype(jnp.float32), axis=0)[:, OVER - MARKS :]
    over = jnp.broadcast_to(over, (8, BLOCK))

    pair = 2 if rows % 2 == 0 else 1
    swap = [(r, r ^ 1) for r in range(rows)]
    hops = range(1, rows // pair)
    shards = [lax.rem(me_row - pair * hop + rows, rows) for hop in range(rows // pair)]
    b_dense = [None] * len(b_stages)

    def across(part, hop):
        return lax.ppermute(part, "row", [(r, (r + pair * hop) % rows) for r in range(rows)])

    def unpack(h, shard, parts, cuts, *tokens):
        stage = b_stages[h]
        flags = parts[0][0, :b_k, :b_columns].astype(jnp.int32)
        b_dense[h], token = unpack_b(
            parts, flags, shard.reshape(1), rows, stage.row, stage.row + stage.rows, b_k, cuts, b_dense[h], tokens
        )
        return token

    came = [across(b_first, hop) for hop in hops]
    cut = [0, b_cuts[-1]]
    token = turn
    for h in range(2):
        token = unpack(h, shards[0], [b_whole], cut, token)
    if pair == 2:
        other = lax.ppermute(b_whole, "row", swap)
        over = jnp.maximum(over, lax.ppermute(over, "row", swap))
        for h in range(2):
            token = unpack(h, shards[0] ^ 1, [other], cut, token, *[over] * h)

    step = pair
    (over,) = after([over], [token])
    while step < rows:
        over = jnp.maximum(over, lax.ppermute(over, "row", [(r, r ^ step) for r in range(rows)]))
        step *= 2
    *came, b_second = after([*came, b_parts[1]], [token, over])
    sides = [[part] for part in came]
    if pair == 2:
        sides += [[lax.ppermute(part, "row", swap)] for part in came]
    came = [across(b_second, hop) for hop in hops]
    places = [shards[hop] ^ side for side in range(pair) for hop in hops]
    for place, parts in zip(places, sides):
        token = unpack(0, place, parts, b_cuts[:2], token)
    def product_of(g, halves, over, **more):
        return multiply(
            a_parts, notes, places_of, (0, 2), a_stages[: g + 1], a_k, a_cuts[: a_counts[g] + 1], halves, over, **more
        )

    def exchange(codes):
        out, high = [], codes.shape[0] // (layers - 1)
        for q in range(layers - 1):
            there = [(i, (i + 1 + q) % layers) for i in range(layers)]
            out.append(lax.ppermute(codes[q * high : (q + 1) * high], "layer", there))
        return out

    (more_a,) = after([more_a], [token, a_parts[1]])
    more_a = round_col(more_a)
    (codes,) = product_of(0, b_dense[:1], over, pieces=layers - 1, remarks=32, tokens=[token])

    came = after(came, [codes, *more_a[1:]])
    a_parts[2] = jnp.stack(more_a)
    first = exchange(codes)
    more = [*came]
    if pair == 2:
        more += [lax.ppermute(part, "row", swap) for part in came]
    for place, parts, part in zip(places, sides, more):
        token = unpack(1, place, [*parts, part], b_cuts, token)
    (codes,) = product_of(0, b_dense[1:], over, pieces=layers - 1, tokens=[token])

    second = exchange(codes)
    (product,) = product_of(1, b_dense, over, tokens=[codes])

    received = [*zip(first, second)]
    product, over = product_of(2, b_dense, over, received=received, before=(product,))
    return lax.cond(
        over[0] > 0,
        lambda: whole_slab(sizes, a_tiles, a_occupancy, b_tiles, b_occupancy),
        lambda: product,
    )


def solution(mesh):
    sizes = tuple(mesh.shape[axis] for axis in ("row", "col", "layer"))
    in_specs = (
        P("row", ("layer", "col")),
        P("row", ("layer", "col")),
        P(("layer", "row"), "col"),
        P(("layer", "row"), "col"),
    )
    out_specs = P(("row", "layer"), "col")
    return jax.shard_map(
        functools.partial(per_device, sizes), mesh=mesh, in_specs=in_specs, out_specs=out_specs, check_vma=False
    )
```
